128 devices in a mesh: ga: 4 (over z), dev: 32 (over y, x, core).
Axes of the slice: x: 4, y: 4, z: 4, core: 2. Of those that a mesh axis runs over, the one named last changes fastest.
Arguments:
- density: float32 [4, 1024, 1024], P(None, 'dev', 'ga'), may hold values from 1 to 2
- velocity: float32 [3, 4, 1024, 1024], P(None, None, 'dev', 'ga'), may hold values from -2.5 to 2.5
- pressure: float32 [4, 1024, 1024], P(None, 'dev', 'ga'), may hold values from 2 to 4
- lift: bfloat16 [3, 32], replicated, may hold values from -32 to 32
- spectral: bfloat16 [64, 2, 32, 32, 128], P('dev'), may hold values from -6 to 6
- pointwise: bfloat16 [32, 32], replicated, may hold values from -1 to 1
- project: bfloat16 [32, 3], replicated, may hold values from -1 to 1
Outputs:
- new_state: float32 [5, 4, 1024, 1024], P(None, None, 'dev', 'ga')
- spectral_grad: float32 [64, 2, 32, 32, 128], P('dev')
The draws below stay inside these ranges and needn't reach their ends.
All inputs are finite; a program needn't handle non-finite values.
Results may differ from the reference program's by a relative error of at most 0.0003.
Values sent between devices are 32-bit elements; how exact they have to be, the bound alone decides.
A program may use at most 128 MiB of HBM per device.

```python
import jax
import jax.numpy as jnp
from jax import lax

WIDTH = 32
MODES = 64
XC = 512
YC = 512
FACTOR = 2
PLANES = 4
NX = 1024
NY = 1024


def levels(key, extent, cuts, low, high):
    loudness, own = 1.0, jax.random.fold_in(key, 6)
    for axis_at, shards_of in cuts:
        heights = jnp.exp(jax.random.uniform(jax.random.fold_in(own, axis_at), (shards_of,), jnp.float32, low / len(cuts), high / len(cuts)))
        loudness = loudness * jnp.repeat(heights, extent[axis_at] // shards_of).reshape([-1 if axis == axis_at else 1 for axis in range(len(extent))])
    return loudness


def normal_values(stream_key, shape, width, most, cuts=(), kind=jnp.bfloat16):
    drawn = jax.random.normal(stream_key, shape, jnp.float32) * width
    if len(cuts) > 0:
        drawn = levels(stream_key, shape, cuts, -0.22, 0.18) * drawn
    return jnp.clip(drawn, min=-most, max=most).astype(kind)


def setup_inputs(seed: int = 0) -> dict:
    streams_of = jax.random.split(jax.random.key(seed), 8)
    density = jnp.clip(1.0 + 1.0 * jax.random.uniform(streams_of[0], (PLANES, NX, NY), jnp.float32) ** levels(streams_of[0], (PLANES, NX, NY), ((1, 32), (2, 4)), -0.2, 0.2), 1.0, 2.0)
    velocity = normal_values(streams_of[1], (3, PLANES, NX, NY), 0.4, 2.5, ((2, 32), (3, 4)), jnp.float32)
    pressure = jnp.clip(2.0 + 2.0 * jax.random.uniform(streams_of[2], (PLANES, NX, NY), jnp.float32) ** levels(streams_of[2], (PLANES, NX, NY), ((1, 32), (2, 4)), -0.2, 0.2), 2.0, 4.0)
    lift = normal_values(streams_of[3], (3, WIDTH), 5.0, 32.0)
    spectral = normal_values(streams_of[4], (MODES, 2, WIDTH, WIDTH, 2 * MODES), 1.0, 6.0, ((0, 32),))
    pointwise = normal_values(streams_of[5], (WIDTH, WIDTH), WIDTH ** -0.5, 1.0)
    project = normal_values(streams_of[6], (WIDTH, 3), WIDTH ** -0.5, 1.0)
    return dict(density=density, velocity=velocity, pressure=pressure, lift=lift, spectral=spectral, pointwise=pointwise, project=project)


gamma_gas = 1.4
time_step = 0.12
block_rows = 64

def primitives(state):
    density = state[0]
    momentum = state[1:4]
    velocity = momentum / density
    pressure = (gamma_gas - 1.0) * (state[4] - 0.5 * lax.optimization_barrier(jnp.sum(momentum * velocity, axis=0)))
    sound = jnp.sqrt(gamma_gas * pressure / density)
    return (velocity, pressure, sound)

def directional(state, velocity, pressure, sound, axis):
    normal = velocity[axis]
    momentum = state[1:4]
    moment_flux = momentum * normal
    moment_flux = moment_flux.at[axis].add(pressure)
    energy_flux = (state[4] + pressure) * normal
    flux = jnp.concatenate([momentum[axis][None], moment_flux, energy_flux[None]], axis=0)
    return (flux, jnp.abs(normal) + sound)

def interface(left, right, flux_left, flux_right, speed_left, speed_right):
    return 0.5 * (flux_left + flux_right) - 0.5 * jnp.maximum(speed_left, speed_right) * (right - left)

def rates(padded):
    velocity, pressure, sound = primitives(padded)
    flux_x, speed_x = directional(padded, velocity, pressure, sound, 1)
    face_x = interface(padded[:, :, :-1, 1:-1], padded[:, :, 1:, 1:-1], flux_x[:, :, :-1, 1:-1], flux_x[:, :, 1:, 1:-1], speed_x[:, :-1, 1:-1], speed_x[:, 1:, 1:-1])
    div_x = face_x[:, :, 1:] - face_x[:, :, :-1]
    flux_y, speed_y = directional(padded, velocity, pressure, sound, 2)
    face_y = interface(padded[:, :, 1:-1, :-1], padded[:, :, 1:-1, 1:], flux_y[:, :, 1:-1, :-1], flux_y[:, :, 1:-1, 1:], speed_y[:, 1:-1, :-1], speed_y[:, 1:-1, 1:])
    div_y = face_y[:, :, :, 1:] - face_y[:, :, :, :-1]
    inner = padded[:, :, 1:-1, 1:-1]
    flux_z, speed_z = directional(inner, velocity[:, :, 1:-1, 1:-1], pressure[:, 1:-1, 1:-1], sound[:, 1:-1, 1:-1], 0)
    face_z = interface(inner, jnp.roll(inner, -1, axis=1), flux_z, jnp.roll(flux_z, -1, axis=1), speed_z, jnp.roll(speed_z, -1, axis=0))
    div_z = face_z - jnp.roll(face_z, 1, axis=1)
    return -(div_x + div_y + div_z)

def all_rates(state):
    padded = jnp.pad(state, ((0, 0), (0, 0), (1, 1), (1, 1)), mode='wrap')
    count = NX // block_rows

    def one_block(index):
        start = (index * block_rows).astype(jnp.int32)
        piece = lax.dynamic_slice_in_dim(padded, start, block_rows + 2, axis=2)
        return rates(piece)
    blocks = lax.map(one_block, jnp.arange(count).astype(jnp.int32))
    return blocks.transpose(1, 2, 0, 3, 4).reshape(5, PLANES, NX, NY)

def coarse_velocity(field):
    shaped = field.reshape(3, PLANES, XC, FACTOR, YC, FACTOR)
    return shaped.mean(axis=(3, 5)).transpose(1, 0, 2, 3)

def trainer_loss(spec_re, spec_im, inputs, targets, lift, pointwise, project):
    highest = lax.Precision.HIGHEST
    hidden = jnp.einsum('bcxy,cw->bwxy', inputs, lift.astype(jnp.float32), precision=highest)
    spectrum = jnp.fft.rfft2(hidden, axes=(2, 3))
    kept = jnp.concatenate([spectrum[:, :, :MODES, :MODES], spectrum[:, :, XC - MODES:, :MODES]], axis=2)
    weight = spec_re + 1j * spec_im
    result = jnp.einsum('biqk,kioq->boqk', kept, weight)
    full = jnp.zeros((PLANES, WIDTH, XC, YC // 2 + 1), kept.dtype)
    full = full.at[:, :, :MODES, :MODES].set(result[:, :, :MODES])
    full = full.at[:, :, XC - MODES:, :MODES].set(result[:, :, MODES:])
    spatial = jnp.fft.irfft2(full, s=(XC, YC), axes=(2, 3))
    pre = jnp.einsum('bixy,io->boxy', hidden, pointwise.astype(jnp.float32), precision=highest) + spatial
    activated = jax.nn.gelu(pre)
    output = jnp.einsum('boxy,oc->bcxy', activated, project.astype(jnp.float32), precision=highest)
    return 0.5 * jnp.sum((output - targets) ** 2)

def reference(density, velocity, pressure, lift, spectral, pointwise, project):
    momentum = density[None] * velocity
    energy = pressure / (gamma_gas - 1.0) + 0.5 * density * lax.optimization_barrier(jnp.sum(velocity * velocity, axis=0))
    state = jnp.concatenate([density[None], momentum, energy[None]], axis=0)
    rate_one = all_rates(state)
    rate_two = all_rates(state + 0.5 * time_step * rate_one)
    rate_three = all_rates(state + 0.5 * time_step * rate_two)
    rate_four = all_rates(state + time_step * rate_three)
    new_state = state + time_step / 6.0 * (rate_one + 2.0 * rate_two + 2.0 * rate_three + rate_four)
    inputs = coarse_velocity(velocity)
    targets = coarse_velocity(new_state[1:4] / new_state[0])
    spec = spectral.astype(jnp.float32)
    grad_re, grad_im = jax.grad(trainer_loss, argnums=(0, 1))(spec[:, 0], spec[:, 1], inputs, targets, lift, pointwise, project)
    return (new_state, jnp.stack([grad_re, grad_im], axis=1))
```

```python
import functools
import math

import jax
import jax.numpy as jnp
import numpy as np
from jax import lax
from jax.experimental import pallas as pl
from jax.experimental.pallas import tpu as pltpu
from jax.sharding import PartitionSpec as P

MESH = pl.DeviceIdType.MESH
F32 = jnp.float32
BF16 = jnp.bfloat16
WIDTH = 32
MODES = 64
XC = 512
YC = 512
GA = 4
DEV = 32
DT = 0.12


def tables():
    ky = np.arange(MODES)
    y = np.arange(YC)
    ang = 2 * np.pi * ((ky[:, None] * y[None, :]) % YC) / YC
    fwd = np.stack([np.cos(ang), -np.sin(ang)], axis=1)
    weight = np.where(ky == 0, 1.0, 2.0) / (XC * YC)
    inv = fwd * weight[:, None, None]
    fwd_dj = fwd.reshape(DEV, 4, YC)
    fwd_jd = fwd_dj.transpose(1, 0, 2).reshape(128, YC)
    inv_jd = inv.reshape(DEV, 4, YC).transpose(1, 0, 2).reshape(128, YC).T
    q = np.arange(2 * MODES)
    kx = np.where(q < MODES, q, XC - 2 * MODES + q)
    ax = 2 * np.pi * ((kx[:, None] * np.arange(XC)[None, :]) % XC) / XC
    cx = np.concatenate([np.cos(ax), np.sin(ax)], axis=0)

    def split(a):
        a = np.asarray(a, np.float32)
        hi = a.astype(jnp.bfloat16)
        lo = (a - hi.astype(np.float32)).astype(jnp.bfloat16)
        return np.ascontiguousarray(np.stack([hi, lo]))

    pool = np.zeros((256, 128), np.float32)
    pool[np.arange(256), np.arange(256) // 2] = 0.25
    return (
        split(fwd_dj.reshape(128, YC)),
        split(fwd_jd),
        split(inv_jd),
        split(cx),
        split(cx.T),
        pool.astype(jnp.bfloat16),
    )


def split2(a):
    hi = a.astype(BF16)
    return hi, (a - hi.astype(F32)).astype(BF16)


def nn(a, b):
    return lax.dot_general(a, b, (((1,), (0,)), ((), ())), preferred_element_type=F32)


def nt(a, b):
    return lax.dot_general(a, b, (((1,), (1,)), ((), ())), preferred_element_type=F32)


def tn(a, b):
    return lax.dot_general(a, b, (((0,), (0,)), ((), ())), preferred_element_type=F32)


def primitives(u):
    inv = 1.0 / u[0]
    v = [u[1] * inv, u[2] * inv, u[3] * inv]
    kinetic = u[1] * v[0] + u[2] * v[1] + u[3] * v[2]
    p = 0.4 * (u[4] - 0.5 * kinetic)
    sound = jnp.sqrt(1.4 * p * inv)
    return v, p, sound


def directional(u, v, p, sound, d):
    n = v[d]
    flux = [u[1 + d]]
    for i in range(3):
        f = u[1 + i] * n
        flux.append(f + p if i == d else f)
    flux.append((u[4] + p) * n)
    return flux, jnp.abs(n) + sound


def faces(ul, ur, fl, fr, sl, sr):
    top = jnp.maximum(sl, sr)
    return [(a + b) - top * (d - c) for a, b, c, d in zip(fl, fr, ul, ur)]


def rim_rates(u):
    v, p, sound = primitives(u)
    total, along_y = None, None
    for d, (axis, step, size) in enumerate(((0, 2, 8), (1, 8, 384), (1, 1, 384))):
        flux, speed = directional(u, v, p, sound, d)

        def up(a):
            return pltpu.roll(a, size - step, axis)

        g = faces(u, [up(a) for a in u], flux, [up(a) for a in flux], speed, up(speed))
        div = [a - pltpu.roll(a, step, axis) for a in g]
        total = div if total is None else [a + b for a, b in zip(total, div)]
        along_y = g
    return total, along_y


def block_rates(src, edge, r0):
    lane = lax.broadcasted_iota(jnp.int32, (4, 8, 128), 2)
    odd = lax.broadcasted_iota(jnp.int32, (4, 8, 128), 1) % 2 == 1
    last = lane == 127
    base = pl.multiple_of(8 * (r0 - 1), 8)
    wide = [src[f, pl.ds(base, 48), :].reshape(6, 8, 128) for f in range(5)]
    v, p, sound = primitives(wide)
    flux, speed = directional(wide, v, p, sound, 1)
    g = faces(
        [a[:5] for a in wide], [a[1:] for a in wide], [a[:5] for a in flux], [a[1:] for a in flux], speed[:5], speed[1:]
    )
    total = [a[1:] - a[:4] for a in g]
    u = [a[1:5] for a in wide]
    v = [a[1:5] for a in v]
    p, sound = p[1:5], sound[1:5]

    flux, speed = directional(u, v, p, sound, 0)

    def up_z(a):
        return pltpu.roll(a, 6, 1)

    g = faces(u, [up_z(a) for a in u], flux, [up_z(a) for a in flux], speed, up_z(speed))
    total = [t + (a - pltpu.roll(a, 2, 1)) for t, a in zip(total, g)]

    flux, speed = directional(u, v, p, sound, 2)

    def up_y(a):
        near = pltpu.roll(a, 127, 2)
        return jnp.where(last, pltpu.roll(near, 7, 1), near)

    g = faces(u, [up_y(a) for a in u], flux, [up_y(a) for a in flux], speed, up_y(speed))
    at = pl.multiple_of(8 * r0, 8)
    for f in range(5):
        outer = edge[f, pl.ds(at, 32), :].reshape(4, 8, 128)
        upper = jnp.where(last & odd, outer, g[f])
        wrapped = jnp.where(odd, pltpu.roll(g[f], 1, 1), outer)
        lower = pltpu.roll(jnp.where(last, wrapped, g[f]), 1, 2)
        total[f] = total[f] + (upper - lower)
    return total


def kernel(
    lift_s, density, velocity, pressure, lift, pointwise, project, spectral_h,
    fdj_h, fjd_h, inv_h, cx_h, cxt_h, pool_h,
    new_state, t_out,
    spectral, fdj, fjd, inv, cx, cxt, pool,
    u0, ua, ub, acc, edge, rim, own_edge, side_edge, row_edge, corner_edge,
    pooled, snd_in, rcv_in, snd_tg, rcv_tg, snd_x, rcv_x, snd_b, rcv_b, snd_g, rcv_g,
    contracted, modes, grads, rt_hi, rt_lo, slope, made, dp_hi, dp_lo, ft, lpx_ref, pxt_ref,
    load_sem, halo_send, halo_recv, in_send, in_recv, tg_send, tg_recv, x_send, x_recv, b_send, b_recv,
    g_send, g_recv, xm_send, xm_recv, gm_send, gm_recv,
):
    ga = lax.axis_index("ga")
    dev = lax.axis_index("dev")
    east, west = lax.rem(ga + 1, GA), lax.rem(ga + GA - 1, GA)
    south, north = lax.rem(dev + 1, DEV), lax.rem(dev + DEV - 1, DEV)

    loads = [
        pltpu.make_async_copy(a, b, load_sem.at[n])
        for n, (a, b) in enumerate(
            ((pool_h, pool), (spectral_h, spectral), (fdj_h, fdj), (cx_h, cx), (cxt_h, cxt), (inv_h, inv), (fjd_h, fjd))
        )
    ]
    for c in loads:
        c.start()

    barrier = pltpu.get_barrier_semaphore()

    def greet(s, carry):
        pl.semaphore_signal(barrier, inc=1, device_id=(ga, lax.rem(dev + s, DEV)), device_id_type=MESH)
        return carry

    lax.fori_loop(1, DEV, greet, 0)
    for s in range(1, GA):
        pl.semaphore_signal(barrier, inc=1, device_id=(lax.rem(ga + s, GA), dev), device_id_type=MESH)
    for a in (east, west):
        for b in (south, north):
            pl.semaphore_signal(barrier, inc=1, device_id=(a, b), device_id_type=MESH)

    def exchange_rows(snd, rcv, ssem, rsem):
        def go(s, carry):
            peer = lax.rem(dev + s, DEV)
            pltpu.make_async_remote_copy(
                src_ref=snd.at[pl.ds(pl.multiple_of(16 * peer, 16), 16)],
                dst_ref=rcv.at[pl.ds(pl.multiple_of(16 * dev, 16), 16)],
                send_sem=ssem.at[peer], recv_sem=rsem.at[dev],
                device_id=(ga, peer), device_id_type=MESH,
            ).start()
            return carry

        lax.fori_loop(1, DEV, go, 0)
        mine = pl.ds(pl.multiple_of(16 * dev, 16), 16)
        rcv[mine, :] = snd[mine, :]

    def wait_rows(snd, rcv, ssem, rsem):
        def go(s, carry):
            peer = lax.rem(dev + s, DEV)
            at = pl.ds(pl.multiple_of(16 * peer, 16), 16)
            pltpu.make_async_remote_copy(
                src_ref=snd.at[at], dst_ref=rcv.at[at], send_sem=ssem.at[peer], recv_sem=rsem.at[peer],
                device_id=(ga, peer), device_id_type=MESH,
            ).wait()
            return carry

        lax.fori_loop(1, DEV, go, 0)

    def across(s, src, dst, ssem, rsem, arriving):
        peer = lax.rem(ga + s, GA)
        return pltpu.make_async_remote_copy(
            src_ref=src(peer), dst_ref=dst(peer if arriving else ga), send_sem=ssem.at[peer],
            recv_sem=rsem.at[peer if arriving else ga], device_id=(peer, dev), device_id_type=MESH,
        )

    def start_across(src, dst, ssem, rsem):
        for s in (1, 3, 2):
            across(s, src, dst, ssem, rsem, False).start()

    def wait_across(src, dst, ssem, rsem):
        for s in (1, 3, 2):
            across(s, src, dst, ssem, rsem, True).wait()

    def coarsen(rows, snd):
        hi, lo = split2(rows)
        pooled[...] = nn(hi, pool[...]) + nn(lo, pool[...])
        both = pooled[pl.ds(0, 192, stride=2), :] + pooled[pl.ds(1, 192, stride=2), :]
        snd[...] = both.reshape(GA, 48, 128)

    for p in range(4):
        for h in range(2):
            cols = slice(128 * h, 128 * h + 128)
            rho = density[p, :, cols]
            v = [velocity[c, p, :, cols] for c in range(3)]
            where = pl.ds(32 + 2 * p + h, 32, stride=8)
            u0[0, where, :] = rho
            for c in range(3):
                u0[1 + c, where, :] = rho * v[c]
            u0[4, where, :] = pressure[p, :, cols] / 0.4 + 0.5 * rho * (v[0] * v[0] + v[1] * v[1] + v[2] * v[2])

    lane1 = lax.broadcasted_iota(jnp.int32, (8, 128), 1)
    for w in range(2):
        for f in range(5):
            packed = None
            for k in range(16):
                row = pltpu.roll(u0[f, pl.ds(8 * (16 * w + k + 4), 8), :], (4 + 8 * k) % 128, 1)
                packed = row if packed is None else jnp.where(lane1 >= 8 * k, row, packed)
            own_edge[w, f] = packed

    loads[0].wait()
    coarsen(jnp.concatenate([velocity[c, p] for p in range(4) for c in range(3)], axis=0), snd_in)

    pl.semaphore_wait(barrier, DEV - 1 + GA - 1 + 4)

    def halo(n, src, dst, target):
        return pltpu.make_async_remote_copy(
            src_ref=src, dst_ref=dst, send_sem=halo_send.at[n], recv_sem=halo_recv.at[n],
            device_id=target, device_id_type=MESH,
        )

    halos = [
        halo(0, u0.at[:, pl.ds(8 * 32, 32)], u0.at[:, pl.ds(0, 32)], (ga, south)),
        halo(1, u0.at[:, pl.ds(8 * 4, 32)], u0.at[:, pl.ds(8 * 36, 32)], (ga, north)),
        halo(2, own_edge.at[1], row_edge.at[0], (ga, south)),
        halo(3, own_edge.at[0], row_edge.at[1], (ga, north)),
        halo(4, own_edge, side_edge.at[0], (east, dev)),
        halo(5, own_edge, side_edge.at[1], (west, dev)),
        halo(6, own_edge.at[1], corner_edge.at[0], (east, south)),
        halo(7, own_edge.at[0], corner_edge.at[1], (east, north)),
        halo(8, own_edge.at[1], corner_edge.at[2], (west, south)),
        halo(9, own_edge.at[0], corner_edge.at[3], (west, north)),
    ]
    in_args = (lambda g: snd_in.at[g], lambda g: rcv_in.at[g], in_send, in_recv)
    start_across(*in_args)
    for c in halos:
        c.start()
    rcv_in[ga] = snd_in[ga]

    loads[1].wait()
    for ky in range(2):
        for part in range(2):

            def add(w8, total, ky=ky, part=part):
                total = list(total)
                for n in range(4):
                    w = 4 * w8 + n
                    s = spectral[ky, part, w].astype(F32)
                    for c in range(3):
                        total[c] = total[c] + lift_s[c, w] * s
                return tuple(total)

            zero = jnp.zeros((WIDTH, 128), F32)
            done = lax.fori_loop(0, WIDTH // 4, add, (zero, zero, zero))
            for c in range(3):
                contracted[ky, part, c] = done[c]

    tile_o = (
        lax.broadcasted_iota(jnp.int32, (WIDTH, 512), 1) % WIDTH == lax.broadcasted_iota(jnp.int32, (WIDTH, 512), 0)
    ).astype(F32).astype(BF16)
    same_row = (
        lax.broadcasted_iota(jnp.int32, (48, 512), 1) // WIDTH == lax.broadcasted_iota(jnp.int32, (48, 512), 0) % 16
    )

    def spread(a):
        return jnp.where(
            same_row, jnp.concatenate([jnp.broadcast_to(a[c : c + 1], (16, 512)) for c in range(3)], axis=0), 0.0
        )

    lp_hi, lp_lo = split2(nn(lift[...], pointwise[...]))
    lpx_ref[...] = spread(nn(lp_hi, tile_o) + nn(lp_lo, tile_o))
    pxt_ref[...] = spread(tn(project[...], tile_o)).astype(BF16)

    wait_across(*in_args)
    loads[2].wait()
    hi, lo = split2(jnp.concatenate([rcv_in[g] for g in range(GA)], axis=1))
    freq = nt(hi, fdj[0]) + nt(hi, fdj[1]) + nt(lo, fdj[0])
    lane2 = lax.broadcasted_iota(jnp.int32, (16, 128), 1)
    for d in range(DEV):
        a, b, c = (pltpu.roll(freq[16 * n : 16 * n + 16], (4 * n - 4 * d) % 128, 1) for n in range(3))
        snd_x[pl.ds(16 * d, 16), :] = jnp.where(lane2 < 4, a, jnp.where(lane2 < 8, b, c))
    x_args = (snd_x, rcv_x, x_send, x_recv)
    exchange_rows(*x_args)

    for c in halos:
        c.wait()
    sub1 = lax.broadcasted_iota(jnp.int32, (8, 128), 0)
    even, first = sub1 % 2 == 0, lane1 % 8 < 4
    low = lane1 < 64
    for f in range(5):
        own = [own_edge[0, f], own_edge[1, f], jnp.where(low, row_edge[1, f], row_edge[0, f])]
        left = [side_edge[0, 0, f], side_edge[0, 1, f], jnp.where(low, corner_edge[1, f], corner_edge[0, f])]
        right = [side_edge[1, 0, f], side_edge[1, 1, f], jnp.where(low, corner_edge[3, f], corner_edge[2, f])]
        for n in range(3):
            rim[0, f, :, 128 * n : 128 * n + 128] = jnp.where(
                even,
                jnp.where(first, pltpu.roll(left[n], 7, 0), own[n]),
                jnp.where(first, own[n], pltpu.roll(right[n], 1, 0)),
            )

    def stage(src, dst, ahead, gain, first_row, blocks, first_stage, rim_src, rim_dst):
        total, along_y = rim_rates([rim[rim_src, f] for f in range(5)])
        for f in range(5):
            if rim_dst is not None:
                rim[rim_dst, f] = rim[0, f] - (0.5 * ahead) * total[f]
            for n in range(3):
                for k in range(16):
                    edge[f, pl.ds(8 * ((16 * n + k + 4) % 48), 8), :] = pltpu.roll(
                        along_y[f][:, 128 * n : 128 * n + 128], 124 - 8 * k, 1
                    )

        def block(n, carry):
            r0 = first_row + 4 * n
            if first_stage:
                r0 = jnp.minimum(r0, 35)
            total = block_rates(src, edge, r0)
            at = pl.ds(pl.multiple_of(8 * r0, 8), 32)
            for f in range(5):
                t = total[f].reshape(32, 128)
                start = u0[f, at, :]
                if dst is not None:
                    dst[f, at, :] = start - (0.5 * ahead) * t
                old = start if first_stage else acc[f, at, :]
                acc[f, at, :] = old - (0.5 * gain) * t
            return carry

        lax.fori_loop(0, blocks, block, 0)

    stage(u0, ua, 0.5 * DT, DT / 6, 1, 10, True, 0, 1)

    wait_rows(*x_args)
    loads[3].wait()
    hi, lo = split2(rcv_x[...])
    turned = nn(cx[0], hi) + nn(cx[1], hi) + nn(cx[0], lo)
    cosine, sine = turned[:128].T, turned[128:].T
    for ky in range(2):
        for c in range(3):
            r = 4 * c + 2 * ky
            modes[ga, 8 * ky + 2 * c : 8 * ky + 2 * c + 1, :] = cosine[r : r + 1] + sine[r + 1 : r + 2]
            modes[ga, 8 * ky + 2 * c + 1 : 8 * ky + 2 * c + 2, :] = cosine[r + 1 : r + 2] - sine[r : r + 1]
        modes[ga, 8 * ky + 6 : 8 * ky + 8, :] = jnp.zeros((2, 128), F32)
    modes_args = (lambda g: modes.at[ga], lambda g: modes.at[g], xm_send, xm_recv)
    start_across(*modes_args)
    mine = modes[ga]
    rows = []
    for ky in range(2):
        out_re, out_im = 0.0, 0.0
        for c in range(3):
            a = mine[8 * ky + 2 * c : 8 * ky + 2 * c + 1]
            b = mine[8 * ky + 2 * c + 1 : 8 * ky + 2 * c + 2]
            re, im = contracted[ky, 0, c], contracted[ky, 1, c]
            out_re = out_re + (a * re - b * im)
            out_im = out_im + (a * im + b * re)
        rows.append(jnp.concatenate([out_re, -out_im], axis=1))
        rows.append(jnp.concatenate([out_im, out_re], axis=1))
    hi, lo = split2(jnp.concatenate(rows, axis=0))
    loads[4].wait()
    snd_b[...] = nt(cxt[0], hi) + nt(cxt[1], hi) + nt(cxt[0], lo)
    b_args = (snd_b, rcv_b, b_send, b_recv)
    exchange_rows(*b_args)

    stage(ua, ub, 0.5 * DT, DT / 3, 2, 9, False, 1, 2)
    stage(ub, ua, DT, DT / 3, 2, 9, False, 2, 1)
    stage(ua, None, DT, DT / 6, 4, 8, False, 1, None)

    after = []
    for p in range(4):
        parts = []
        for h in range(2):
            where = pl.ds(32 + 2 * p + h, 32, stride=8)
            cols = slice(128 * h, 128 * h + 128)
            u = [acc[f, where, :] for f in range(5)]
            for f in range(5):
                new_state[f, p, :, cols] = u[f]
            inv_rho = 1.0 / u[0]
            parts.append([u[1 + c] * inv_rho for c in range(3)])
        for c in range(3):
            after.append(jnp.concatenate([parts[0][c], parts[1][c]], axis=1))
    coarsen(jnp.concatenate(after, axis=0), snd_tg)
    tg_args = (lambda g: snd_tg.at[g], lambda g: rcv_tg.at[g], tg_send, tg_recv)
    start_across(*tg_args)
    rcv_tg[ga] = snd_tg[ga]

    wait_rows(*b_args)
    loads[5].wait()
    group = lax.broadcasted_iota(jnp.int32, (32, 128), 1) // 32
    for t in range(4):
        src = [rcv_b[pl.ds(4 * t + m, 32, stride=16), :] for m in range(4)]
        for j in range(4):
            made_of = None
            for m in range(4):
                turn = (32 * (m - j)) % 128
                piece = pltpu.roll(src[m], turn, 1) if turn else src[m]
                made_of = piece if made_of is None else jnp.where(group == m, piece, made_of)
            hi, lo = split2(made_of)
            rt_hi[pl.ds(32 * j, 32), 128 * t : 128 * t + 128] = hi
            rt_lo[pl.ds(32 * j, 32), 128 * t : 128 * t + 128] = lo

    lpx_hi, lpx_lo = split2(lpx_ref[...])
    k0, k1 = math.sqrt(2.0 / math.pi), 0.044715

    def transposed(a):
        a = jnp.concatenate([a, jnp.zeros((80, 128), F32)], axis=0)
        return a.T[:, :48]

    def forward(g, carry):
        at = pl.ds(pl.multiple_of(128 * g, 128), 128)
        ins_hi, ins_lo = split2(transposed(rcv_in[g]))
        pre = nn(inv[0, at, :], rt_hi[...]) + nn(inv[1, at, :], rt_hi[...]) + nn(inv[0, at, :], rt_lo[...])
        pre = pre + nn(ins_hi, lpx_hi) + nn(ins_hi, lpx_lo) + nn(ins_lo, lpx_hi)
        square = pre * pre
        t = jnp.tanh(k0 * pre * (1.0 + k1 * square))
        half = 0.5 * (1.0 + t)
        slope[at, :] = half + (0.5 * k0) * pre * (1.0 - t * t) * (1.0 + (3.0 * k1) * square)
        hi, lo = split2(pre * half)
        made[at, :] = nt(hi, pxt_ref[...]) + nt(lo, pxt_ref[...])
        return carry

    lax.fori_loop(0, GA, forward, 0)

    wait_across(*tg_args)

    def backward(g, carry):
        at = pl.ds(pl.multiple_of(128 * g, 128), 128)
        hi, lo = split2(made[at, :] - transposed(rcv_tg[g]))
        d_pre = (nn(hi, pxt_ref[...]) + nn(lo, pxt_ref[...])) * slope[at, :]
        hi, lo = split2(d_pre)
        dp_hi[at, :] = hi
        dp_lo[at, :] = lo
        return carry

    lax.fori_loop(0, GA, backward, 0)
    loads[6].wait()
    for t in range(4):
        cols = slice(128 * t, 128 * t + 128)
        ft[t] = nn(fjd[0], dp_hi[:, cols]) + nn(fjd[1], dp_hi[:, cols]) + nn(fjd[0], dp_lo[:, cols])
    for t in range(4):
        src = [ft[t, pl.ds(32 * j, 32), :] for j in range(4)]
        for m in range(4):
            made_of = None
            for j in range(4):
                turn = (32 * (j - m)) % 128
                piece = pltpu.roll(src[j], turn, 1) if turn else src[j]
                made_of = piece if made_of is None else jnp.where(group == j, piece, made_of)
            snd_g[pl.ds(4 * t + m, 32, stride=16), :] = made_of
    g_args = (snd_g, rcv_g, g_send, g_recv)
    exchange_rows(*g_args)
    wait_rows(*g_args)

    hi, lo = split2(rcv_g[...])
    turned = nn(cx[0], hi) + nn(cx[1], hi) + nn(cx[0], lo)
    cosine, sine = turned[:128].T, turned[128:].T
    for ky in range(2):
        re, im = slice(64 * ky, 64 * ky + 32), slice(64 * ky + 32, 64 * ky + 64)
        grads[ga, ky, 0] = cosine[re] + sine[im]
        grads[ga, ky, 1] = cosine[im] - sine[re]
    grads_args = (lambda g: grads.at[ga], lambda g: grads.at[g], gm_send, gm_recv)
    start_across(*grads_args)
    wait_across(*modes_args)
    wait_across(*grads_args)
    for ky in range(2):
        factor = jnp.where(2 * dev + ky == 0, 1.0, 2.0).astype(F32) / (XC * YC)
        for c in range(3):
            out_re, out_im = 0.0, 0.0
            for b in range(GA):
                x_re = modes[b, 8 * ky + 2 * c : 8 * ky + 2 * c + 1, :]
                x_im = modes[b, 8 * ky + 2 * c + 1 : 8 * ky + 2 * c + 2, :]
                g_re, g_im = grads[b, ky, 0], grads[b, ky, 1]
                out_re = out_re + (x_re * g_re + x_im * g_im)
                out_im = out_im + (x_re * g_im - x_im * g_re)
            t_out[ky, 0, c] = out_re * factor
            t_out[ky, 1, c] = out_im * factor


def expand_kernel(lift_s, t_ref, out_ref):
    part = [t_ref[0, 0, c] for c in range(3)]
    for i in range(WIDTH):
        out_ref[0, 0, i] = lift_s[0, i] * part[0] + lift_s[1, i] * part[1] + lift_s[2, i] * part[2]


def per_device(consts, density, velocity, pressure, lift, spectral, pointwise, project):
    lift_f = lift.astype(F32)
    vmem = pl.BlockSpec(memory_space=pltpu.VMEM)
    smem = pl.BlockSpec(memory_space=pltpu.SMEM)
    hbm = pl.BlockSpec(memory_space=pl.ANY)
    V = pltpu.VMEM
    dma = pltpu.SemaphoreType.DMA
    field = V((5, 384, 128), F32)
    rows = V((512, 128), F32)
    coarse = V((GA, 48, 128), F32)
    scratch = [
        V((2, 2, WIDTH, WIDTH, 128), BF16), V((2, 128, 512), BF16), V((2, 128, 512), BF16), V((2, 512, 128), BF16),
        V((2, 256, 512), BF16), V((2, 512, 256), BF16), V((256, 128), BF16),
        field, field, field, field, field, V((3, 5, 8, 384), F32),
        V((2, 5, 8, 128), F32), V((2, 2, 5, 8, 128), F32), V((2, 5, 8, 128), F32), V((4, 5, 8, 128), F32),
        V((384, 128), F32), coarse, coarse, coarse, coarse, rows, rows, rows, rows, rows, rows,
        V((2, 2, 3, WIDTH, 128), F32), V((GA, 16, 128), F32), V((GA, 2, 2, WIDTH, 128), F32),
        V((128, 512), BF16), V((128, 512), BF16), V((512, 512), F32), V((512, 48), F32),
        V((512, 512), BF16), V((512, 512), BF16), V((4, 128, 128), F32), V((48, 512), F32), V((48, 512), BF16),
        dma((7,)), dma((10,)), dma((10,)), dma((GA,)), dma((GA,)), dma((GA,)), dma((GA,)),
        dma((DEV,)), dma((DEV,)), dma((DEV,)), dma((DEV,)), dma((DEV,)), dma((DEV,)),
        dma((GA,)), dma((GA,)), dma((GA,)), dma((GA,)),
    ]
    new_state, t = pl.pallas_call(
        kernel,
        out_shape=(
            jax.ShapeDtypeStruct((5, 4, 32, 256), F32),
            jax.ShapeDtypeStruct((2, 2, 3, WIDTH, 128), F32),
        ),
        in_specs=[smem] + [vmem] * 6 + [hbm] * 7,
        out_specs=(vmem, vmem),
        scratch_shapes=scratch,
        compiler_params=pltpu.CompilerParams(
            collective_id=0, has_side_effects=True, vmem_limit_bytes=44 * 1024 * 1024
        ),
    )(lift_f, density, velocity, pressure, lift, pointwise, project, spectral, *consts)
    grad = pl.pallas_call(
        expand_kernel,
        grid=(2, 2),
        out_shape=jax.ShapeDtypeStruct((2, 2, WIDTH, WIDTH, 128), F32),
        in_specs=[smem, pl.BlockSpec((1, 1, 3, WIDTH, 128), lambda a, b: (a, b, 0, 0, 0))],
        out_specs=pl.BlockSpec((1, 1, WIDTH, WIDTH, 128), lambda a, b: (a, b, 0, 0, 0)),
    )(lift_f, t)
    return new_state, grad


def solution(mesh):
    in_specs = (
        P(None, "dev", "ga"),
        P(None, None, "dev", "ga"),
        P(None, "dev", "ga"),
        P(),
        P("dev", None, None, None, None),
        P(),
        P(),
    )
    out_specs = (P(None, None, "dev", "ga"), P("dev", None, None, None, None))

    def whole(*args):
        consts = tables()
        return jax.shard_map(
            lambda *a: per_device(a[:6], *a[6:]),
            mesh=mesh, in_specs=(P(),) * 6 + in_specs, out_specs=out_specs, check_vma=False,
        )(*[jnp.asarray(c) for c in consts], *args)

    return whole
```

```python
import functools
import math

import jax
import jax.numpy as jnp
import numpy as np
from jax import lax
from jax.experimental import pallas as pl
from jax.experimental.pallas import tpu as pltpu
from jax.sharding import PartitionSpec as P

MESH = pl.DeviceIdType.MESH
F32 = jnp.float32
BF16 = jnp.bfloat16
WIDTH = 32
MODES = 64
XC = 512
YC = 512
GA = 4
DEV = 32
DT = 0.12
VMEM_BYTES = 62 * 1024 * 1024


def tables():
    ky = np.arange(MODES)
    y = np.arange(YC)
    ang = 2 * np.pi * ((ky[:, None] * y[None, :]) % YC) / YC
    fwd = np.stack([np.cos(ang), -np.sin(ang)], axis=1)
    weight = np.where(ky == 0, 1.0, 2.0) / (XC * YC)
    inv = fwd * weight[:, None, None]
    fwd_dj = fwd.reshape(DEV, 4, YC)
    fwd_jd = fwd_dj.transpose(1, 0, 2).reshape(128, YC)
    inv_jd = inv.reshape(DEV, 4, YC).transpose(1, 0, 2).reshape(128, YC).T
    q = np.arange(2 * MODES)
    kx = np.where(q < MODES, q, XC - 2 * MODES + q)
    ax = 2 * np.pi * ((kx[:, None] * np.arange(XC)[None, :]) % XC) / XC
    cx = np.concatenate([np.cos(ax), np.sin(ax)], axis=0)

    def split(a):
        a = np.asarray(a, np.float32)
        hi = a.astype(jnp.bfloat16)
        lo = (a - hi.astype(np.float32)).astype(jnp.bfloat16)
        return np.ascontiguousarray(np.stack([hi, lo]))

    pool = np.zeros((256, 128), np.float32)
    pool[np.arange(256), np.arange(256) // 2] = 0.25
    return (
        split(fwd_dj.reshape(128, YC)),
        split(fwd_jd),
        split(inv_jd),
        split(cx),
        split(cx.T),
        pool.astype(jnp.bfloat16),
    )


def split2(a):
    hi = a.astype(BF16)
    return hi, (a - hi.astype(F32)).astype(BF16)


def nn(a, b):
    return lax.dot_general(a, b, (((1,), (0,)), ((), ())), preferred_element_type=F32)


def nt(a, b):
    return lax.dot_general(a, b, (((1,), (1,)), ((), ())), preferred_element_type=F32)


def tn(a, b):
    return lax.dot_general(a, b, (((0,), (0,)), ((), ())), preferred_element_type=F32)


def primitives(u):
    inv = 1.0 / u[0]
    v = [u[1] * inv, u[2] * inv, u[3] * inv]
    kinetic = u[1] * v[0] + u[2] * v[1] + u[3] * v[2]
    p = 0.4 * (u[4] - 0.5 * kinetic)
    sound = jnp.sqrt(1.4 * p * inv)
    return v, p, sound


def directional(u, v, p, sound, d):
    n = v[d]
    flux = [u[1 + d]]
    for i in range(3):
        f = u[1 + i] * n
        flux.append(f + p if i == d else f)
    flux.append((u[4] + p) * n)
    return flux, jnp.abs(n) + sound


def faces(ul, ur, fl, fr, sl, sr):
    top = jnp.maximum(sl, sr)
    return [(a + b) - top * (d - c) for a, b, c, d in zip(fl, fr, ul, ur)]


def widened(lift, c):
    pick = (lax.broadcasted_iota(jnp.int32, (3, 128), 0) == c).astype(F32).astype(BF16)
    return tn(lift, pick)


def rim_rates(u):
    v, p, sound = primitives(u)
    total, along_y = None, None
    for d, (axis, step, size) in enumerate(((0, 2, 8), (1, 8, 384), (1, 1, 384))):
        flux, speed = directional(u, v, p, sound, d)

        def up(a):
            return pltpu.roll(a, size - step, axis)

        g = faces(u, [up(a) for a in u], flux, [up(a) for a in flux], speed, up(speed))
        div = [a - pltpu.roll(a, step, axis) for a in g]
        total = div if total is None else [a + b for a, b in zip(total, div)]
        along_y = g
    return total, along_y


def block_rates(src, edge, r0):
    lane = lax.broadcasted_iota(jnp.int32, (4, 8, 128), 2)
    odd = lax.broadcasted_iota(jnp.int32, (4, 8, 128), 1) % 2 == 1
    last = lane == 127
    base = pl.multiple_of(8 * (r0 - 1), 8)
    wide = [src[f, pl.ds(base, 48), :].reshape(6, 8, 128) for f in range(5)]
    v, p, sound = primitives(wide)
    flux, speed = directional(wide, v, p, sound, 1)
    g = faces(
        [a[:5] for a in wide], [a[1:] for a in wide], [a[:5] for a in flux], [a[1:] for a in flux], speed[:5], speed[1:]
    )
    total = [a[1:] - a[:4] for a in g]
    u = [a[1:5] for a in wide]
    v = [a[1:5] for a in v]
    p, sound = p[1:5], sound[1:5]

    flux, speed = directional(u, v, p, sound, 0)

    def up_z(a):
        return pltpu.roll(a, 6, 1)

    g = faces(u, [up_z(a) for a in u], flux, [up_z(a) for a in flux], speed, up_z(speed))
    total = [t + (a - pltpu.roll(a, 2, 1)) for t, a in zip(total, g)]

    flux, speed = directional(u, v, p, sound, 2)

    def up_y(a):
        near = pltpu.roll(a, 127, 2)
        return jnp.where(last, pltpu.roll(near, 7, 1), near)

    g = faces(u, [up_y(a) for a in u], flux, [up_y(a) for a in flux], speed, up_y(speed))
    at = pl.multiple_of(8 * r0, 8)
    for f in range(5):
        outer = edge[f, pl.ds(at, 32), :].reshape(4, 8, 128)
        upper = jnp.where(last & odd, outer, g[f])
        wrapped = jnp.where(odd, pltpu.roll(g[f], 1, 1), outer)
        lower = pltpu.roll(jnp.where(last, wrapped, g[f]), 1, 2)
        total[f] = total[f] + (upper - lower)
    return total


def kernel(
    density_h, velocity_h, pressure_h, lift_h, pointwise_h, project_h, spectral_h,
    fdj_h, fjd_h, inv_h, cx_h, cxt_h, pool_h,
    new_state_h, t_out,
    density, velocity, pressure, lift, pointwise, project, new_state, lift_wide,
    spectral, fdj, fjd, inv, cx, cxt, pool,
    u0, ua, ub, acc, edge, rim, own_edge, side_edge, row_edge, corner_edge,
    pooled, snd_in, rcv_in, snd_tg, rcv_tg, snd_x, rcv_x, snd_b, rcv_b, snd_g, rcv_g,
    contracted, modes, grads, rt_hi, rt_lo, slope, made, dp_hi, dp_lo, ft, lpx_ref, pxt_ref,
    load_sem, halo_send, halo_recv, in_send, in_recv, tg_send, tg_recv, x_send, x_recv, b_send, b_recv,
    g_send, g_recv, xm_send, xm_recv, gm_send, gm_recv,
):
    ga = lax.axis_index("ga")
    dev = lax.axis_index("dev")
    east, west = lax.rem(ga + 1, GA), lax.rem(ga + GA - 1, GA)
    south, north = lax.rem(dev + 1, DEV), lax.rem(dev + DEV - 1, DEV)

    loads = [
        pltpu.make_async_copy(a, b, load_sem.at[n])
        for n, (a, b) in enumerate(
            (
                (pool_h, pool), (spectral_h, spectral), (fdj_h, fdj), (cx_h, cx), (cxt_h, cxt), (inv_h, inv), (fjd_h, fjd),
                (density_h, density), (velocity_h, velocity), (pressure_h, pressure),
                (lift_h, lift), (pointwise_h, pointwise), (project_h, project),
            )
        )
    ]
    for n in (7, 8, 9, 0, 10, 11, 12, 1, 2, 3, 4, 5, 6):
        loads[n].start()

    barrier = pltpu.get_barrier_semaphore()

    def greet(s, carry):
        pl.semaphore_signal(barrier, inc=1, device_id=(ga, lax.rem(dev + s, DEV)), device_id_type=MESH)
        return carry

    lax.fori_loop(1, DEV, greet, 0)
    for s in range(1, GA):
        pl.semaphore_signal(barrier, inc=1, device_id=(lax.rem(ga + s, GA), dev), device_id_type=MESH)
    for a in (east, west):
        for b in (south, north):
            pl.semaphore_signal(barrier, inc=1, device_id=(a, b), device_id_type=MESH)

    def exchange_rows(snd, rcv, ssem, rsem):
        def go(s, carry):
            peer = lax.rem(dev + s, DEV)
            pltpu.make_async_remote_copy(
                src_ref=snd.at[pl.ds(pl.multiple_of(16 * peer, 16), 16)],
                dst_ref=rcv.at[pl.ds(pl.multiple_of(16 * dev, 16), 16)],
                send_sem=ssem.at[peer], recv_sem=rsem.at[dev],
                device_id=(ga, peer), device_id_type=MESH,
            ).start()
            return carry

        lax.fori_loop(1, DEV, go, 0)
        mine = pl.ds(pl.multiple_of(16 * dev, 16), 16)
        rcv[mine, :] = snd[mine, :]

    def wait_rows(snd, rcv, ssem, rsem):
        def go(s, carry):
            peer = lax.rem(dev + s, DEV)
            at = pl.ds(pl.multiple_of(16 * peer, 16), 16)
            pltpu.make_async_remote_copy(
                src_ref=snd.at[at], dst_ref=rcv.at[at], send_sem=ssem.at[peer], recv_sem=rsem.at[peer],
                device_id=(ga, peer), device_id_type=MESH,
            ).wait()
            return carry

        lax.fori_loop(1, DEV, go, 0)

    def across(s, src, dst, ssem, rsem, arriving):
        peer = lax.rem(ga + s, GA)
        return pltpu.make_async_remote_copy(
            src_ref=src(peer), dst_ref=dst(peer if arriving else ga), send_sem=ssem.at[peer],
            recv_sem=rsem.at[peer if arriving else ga], device_id=(peer, dev), device_id_type=MESH,
        )

    def start_across(src, dst, ssem, rsem):
        for s in (1, 3, 2):
            across(s, src, dst, ssem, rsem, False).start()

    def wait_across(src, dst, ssem, rsem):
        for s in (1, 3, 2):
            across(s, src, dst, ssem, rsem, True).wait()

    def coarsen(rows, snd):
        hi, lo = split2(rows)
        pooled[...] = nn(hi, pool[...]) + nn(lo, pool[...])
        both = pooled[pl.ds(0, 192, stride=2), :] + pooled[pl.ds(1, 192, stride=2), :]
        snd[...] = both.reshape(GA, 48, 128)

    for n in (7, 8, 9):
        loads[n].wait()
    for p in range(4):
        for h in range(2):
            cols = slice(128 * h, 128 * h + 128)
            rho = density[p, :, cols]
            v = [velocity[c, p, :, cols] for c in range(3)]
            where = pl.ds(32 + 2 * p + h, 32, stride=8)
            u0[0, where, :] = rho
            for c in range(3):
                u0[1 + c, where, :] = rho * v[c]
            u0[4, where, :] = pressure[p, :, cols] / 0.4 + 0.5 * rho * (v[0] * v[0] + v[1] * v[1] + v[2] * v[2])

    lane1 = lax.broadcasted_iota(jnp.int32, (8, 128), 1)
    for w in range(2):
        for f in range(5):
            packed = None
            for k in range(16):
                row = pltpu.roll(u0[f, pl.ds(8 * (16 * w + k + 4), 8), :], (4 + 8 * k) % 128, 1)
                packed = row if packed is None else jnp.where(lane1 >= 8 * k, row, packed)
            own_edge[w, f] = packed

    loads[0].wait()
    coarsen(jnp.concatenate([velocity[c, p] for p in range(4) for c in range(3)], axis=0), snd_in)

    pl.semaphore_wait(barrier, DEV - 1 + GA - 1 + 4)

    def halo(n, src, dst, target):
        return pltpu.make_async_remote_copy(
            src_ref=src, dst_ref=dst, send_sem=halo_send.at[n], recv_sem=halo_recv.at[n],
            device_id=target, device_id_type=MESH,
        )

    halos = [
        halo(0, u0.at[:, pl.ds(8 * 32, 32)], u0.at[:, pl.ds(0, 32)], (ga, south)),
        halo(1, u0.at[:, pl.ds(8 * 4, 32)], u0.at[:, pl.ds(8 * 36, 32)], (ga, north)),
        halo(2, own_edge.at[1], row_edge.at[0], (ga, south)),
        halo(3, own_edge.at[0], row_edge.at[1], (ga, north)),
        halo(4, own_edge, side_edge.at[0], (east, dev)),
        halo(5, own_edge, side_edge.at[1], (west, dev)),
        halo(6, own_edge.at[1], corner_edge.at[0], (east, south)),
        halo(7, own_edge.at[0], corner_edge.at[1], (east, north)),
        halo(8, own_edge.at[1], corner_edge.at[2], (west, south)),
        halo(9, own_edge.at[0], corner_edge.at[3], (west, north)),
    ]
    in_args = (lambda g: snd_in.at[g], lambda g: rcv_in.at[g], in_send, in_recv)
    start_across(*in_args)
    for c in halos:
        c.start()
    rcv_in[ga] = snd_in[ga]

    for n in (10, 11, 12, 1):
        loads[n].wait()
    for c in range(3):
        lift_wide[c] = widened(lift[...], c)
    for ky in range(2):
        for part in range(2):

            def add(w8, total, ky=ky, part=part):
                total = list(total)
                for n in range(4):
                    w = 4 * w8 + n
                    s = spectral[ky, part, w].astype(F32)
                    for c in range(3):
                        total[c] = total[c] + jnp.broadcast_to(lift_wide[c, pl.ds(w, 1), :], (WIDTH, 128)) * s
                return tuple(total)

            zero = jnp.zeros((WIDTH, 128), F32)
            done = lax.fori_loop(0, WIDTH // 4, add, (zero, zero, zero))
            for c in range(3):
                contracted[ky, part, c] = done[c]

    tile_o = (
        lax.broadcasted_iota(jnp.int32, (WIDTH, 512), 1) % WIDTH == lax.broadcasted_iota(jnp.int32, (WIDTH, 512), 0)
    ).astype(F32).astype(BF16)
    same_row = (
        lax.broadcasted_iota(jnp.int32, (48, 512), 1) // WIDTH == lax.broadcasted_iota(jnp.int32, (48, 512), 0) % 16
    )

    def spread(a):
        return jnp.where(
            same_row, jnp.concatenate([jnp.broadcast_to(a[c : c + 1], (16, 512)) for c in range(3)], axis=0), 0.0
        )

    lp_hi, lp_lo = split2(nn(lift[...], pointwise[...]))
    lpx_ref[...] = spread(nn(lp_hi, tile_o) + nn(lp_lo, tile_o))
    pxt_ref[...] = spread(nn(project[...], tile_o)).astype(BF16)

    wait_across(*in_args)
    loads[2].wait()
    hi, lo = split2(jnp.concatenate([rcv_in[g] for g in range(GA)], axis=1))
    freq = nt(hi, fdj[0]) + nt(hi, fdj[1]) + nt(lo, fdj[0])
    lane2 = lax.broadcasted_iota(jnp.int32, (16, 128), 1)
    for d in range(DEV):
        a, b, c = (pltpu.roll(freq[16 * n : 16 * n + 16], (4 * n - 4 * d) % 128, 1) for n in range(3))
        snd_x[pl.ds(16 * d, 16), :] = jnp.where(lane2 < 4, a, jnp.where(lane2 < 8, b, c))
    x_args = (snd_x, rcv_x, x_send, x_recv)
    exchange_rows(*x_args)

    for c in halos:
        c.wait()
    sub1 = lax.broadcasted_iota(jnp.int32, (8, 128), 0)
    even, first = sub1 % 2 == 0, lane1 % 8 < 4
    low = lane1 < 64
    for f in range(5):
        own = [own_edge[0, f], own_edge[1, f], jnp.where(low, row_edge[1, f], row_edge[0, f])]
        left = [side_edge[0, 0, f], side_edge[0, 1, f], jnp.where(low, corner_edge[1, f], corner_edge[0, f])]
        right = [side_edge[1, 0, f], side_edge[1, 1, f], jnp.where(low, corner_edge[3, f], corner_edge[2, f])]
        for n in range(3):
            rim[0, f, :, 128 * n : 128 * n + 128] = jnp.where(
                even,
                jnp.where(first, pltpu.roll(left[n], 7, 0), own[n]),
                jnp.where(first, own[n], pltpu.roll(right[n], 1, 0)),
            )

    def stage(src, dst, ahead, gain, first_row, blocks, first_stage, rim_src, rim_dst):
        total, along_y = rim_rates([rim[rim_src, f] for f in range(5)])
        for f in range(5):
            if rim_dst is not None:
                rim[rim_dst, f] = rim[0, f] - (0.5 * ahead) * total[f]
            for n in range(3):
                for k in range(16):
                    edge[f, pl.ds(8 * ((16 * n + k + 4) % 48), 8), :] = pltpu.roll(
                        along_y[f][:, 128 * n : 128 * n + 128], 124 - 8 * k, 1
                    )

        def block(n, carry):
            r0 = first_row + 4 * n
            if first_stage:
                r0 = jnp.minimum(r0, 35)
            total = block_rates(src, edge, r0)
            at = pl.ds(pl.multiple_of(8 * r0, 8), 32)
            for f in range(5):
                t = total[f].reshape(32, 128)
                start = u0[f, at, :]
                if dst is not None:
                    dst[f, at, :] = start - (0.5 * ahead) * t
                old = start if first_stage else acc[f, at, :]
                acc[f, at, :] = old - (0.5 * gain) * t
            return carry

        lax.fori_loop(0, blocks, block, 0)

    stage(u0, ua, 0.5 * DT, DT / 6, 1, 10, True, 0, 1)

    wait_rows(*x_args)
    loads[3].wait()
    hi, lo = split2(rcv_x[...])
    turned = nn(cx[0], hi) + nn(cx[1], hi) + nn(cx[0], lo)
    cosine, sine = turned[:128].T, turned[128:].T
    for ky in range(2):
        for c in range(3):
            r = 4 * c + 2 * ky
            modes[ga, 8 * ky + 2 * c : 8 * ky + 2 * c + 1, :] = cosine[r : r + 1] + sine[r + 1 : r + 2]
            modes[ga, 8 * ky + 2 * c + 1 : 8 * ky + 2 * c + 2, :] = cosine[r + 1 : r + 2] - sine[r : r + 1]
        modes[ga, 8 * ky + 6 : 8 * ky + 8, :] = jnp.zeros((2, 128), F32)
    modes_args = (lambda g: modes.at[ga], lambda g: modes.at[g], xm_send, xm_recv)
    start_across(*modes_args)
    mine = modes[ga]
    rows = []
    for ky in range(2):
        out_re, out_im = 0.0, 0.0
        for c in range(3):
            a = mine[8 * ky + 2 * c : 8 * ky + 2 * c + 1]
            b = mine[8 * ky + 2 * c + 1 : 8 * ky + 2 * c + 2]
            re, im = contracted[ky, 0, c], contracted[ky, 1, c]
            out_re = out_re + (a * re - b * im)
            out_im = out_im + (a * im + b * re)
        rows.append(jnp.concatenate([out_re, -out_im], axis=1))
        rows.append(jnp.concatenate([out_im, out_re], axis=1))
    hi, lo = split2(jnp.concatenate(rows, axis=0))
    loads[4].wait()
    snd_b[...] = nt(cxt[0], hi) + nt(cxt[1], hi) + nt(cxt[0], lo)
    b_args = (snd_b, rcv_b, b_send, b_recv)
    exchange_rows(*b_args)

    stage(ua, ub, 0.5 * DT, DT / 3, 2, 9, False, 1, 2)
    stage(ub, ua, DT, DT / 3, 2, 9, False, 2, 1)
    stage(ua, None, DT, DT / 6, 4, 8, False, 1, None)

    after = []
    for p in range(4):
        parts = []
        for h in range(2):
            where = pl.ds(32 + 2 * p + h, 32, stride=8)
            cols = slice(128 * h, 128 * h + 128)
            u = [acc[f, where, :] for f in range(5)]
            for f in range(5):
                new_state[f, p, :, cols] = u[f]
            inv_rho = 1.0 / u[0]
            parts.append([u[1 + c] * inv_rho for c in range(3)])
        for c in range(3):
            after.append(jnp.concatenate([parts[0][c], parts[1][c]], axis=1))
    coarsen(jnp.concatenate(after, axis=0), snd_tg)
    state_copy = pltpu.make_async_copy(new_state, new_state_h, load_sem.at[13])
    state_copy.start()
    tg_args = (lambda g: snd_tg.at[g], lambda g: rcv_tg.at[g], tg_send, tg_recv)
    start_across(*tg_args)
    rcv_tg[ga] = snd_tg[ga]

    wait_rows(*b_args)
    loads[5].wait()
    group = lax.broadcasted_iota(jnp.int32, (32, 128), 1) // 32
    for t in range(4):
        src = [rcv_b[pl.ds(4 * t + m, 32, stride=16), :] for m in range(4)]
        for j in range(4):
            made_of = None
            for m in range(4):
                turn = (32 * (m - j)) % 128
                piece = pltpu.roll(src[m], turn, 1) if turn else src[m]
                made_of = piece if made_of is None else jnp.where(group == m, piece, made_of)
            hi, lo = split2(made_of)
            rt_hi[pl.ds(32 * j, 32), 128 * t : 128 * t + 128] = hi
            rt_lo[pl.ds(32 * j, 32), 128 * t : 128 * t + 128] = lo

    lpx_hi, lpx_lo = split2(lpx_ref[...])
    k0, k1 = math.sqrt(2.0 / math.pi), 0.044715

    def transposed(a):
        a = jnp.concatenate([a, jnp.zeros((80, 128), F32)], axis=0)
        return a.T[:, :48]

    def forward(g, carry):
        at = pl.ds(pl.multiple_of(128 * g, 128), 128)
        ins_hi, ins_lo = split2(transposed(rcv_in[g]))
        pre = nn(inv[0, at, :], rt_hi[...]) + nn(inv[1, at, :], rt_hi[...]) + nn(inv[0, at, :], rt_lo[...])
        pre = pre + nn(ins_hi, lpx_hi) + nn(ins_hi, lpx_lo) + nn(ins_lo, lpx_hi)
        square = pre * pre
        t = jnp.tanh(k0 * pre * (1.0 + k1 * square))
        half = 0.5 * (1.0 + t)
        slope[at, :] = half + (0.5 * k0) * pre * (1.0 - t * t) * (1.0 + (3.0 * k1) * square)
        hi, lo = split2(pre * half)
        made[at, :] = nt(hi, pxt_ref[...]) + nt(lo, pxt_ref[...])
        return carry

    lax.fori_loop(0, GA, forward, 0)

    wait_across(*tg_args)

    def backward(g, carry):
        at = pl.ds(pl.multiple_of(128 * g, 128), 128)
        hi, lo = split2(made[at, :] - transposed(rcv_tg[g]))
        d_pre = (nn(hi, pxt_ref[...]) + nn(lo, pxt_ref[...])) * slope[at, :]
        hi, lo = split2(d_pre)
        dp_hi[at, :] = hi
        dp_lo[at, :] = lo
        return carry

    lax.fori_loop(0, GA, backward, 0)
    loads[6].wait()
    for t in range(4):
        cols = slice(128 * t, 128 * t + 128)
        ft[t] = nn(fjd[0], dp_hi[:, cols]) + nn(fjd[1], dp_hi[:, cols]) + nn(fjd[0], dp_lo[:, cols])
    for t in range(4):
        src = [ft[t, pl.ds(32 * j, 32), :] for j in range(4)]
        for m in range(4):
            made_of = None
            for j in range(4):
                turn = (32 * (j - m)) % 128
                piece = pltpu.roll(src[j], turn, 1) if turn else src[j]
                made_of = piece if made_of is None else jnp.where(group == j, piece, made_of)
            snd_g[pl.ds(4 * t + m, 32, stride=16), :] = made_of
    g_args = (snd_g, rcv_g, g_send, g_recv)
    exchange_rows(*g_args)
    wait_rows(*g_args)

    hi, lo = split2(rcv_g[...])
    turned = nn(cx[0], hi) + nn(cx[1], hi) + nn(cx[0], lo)
    cosine, sine = turned[:128].T, turned[128:].T
    for ky in range(2):
        re, im = slice(64 * ky, 64 * ky + 32), slice(64 * ky + 32, 64 * ky + 64)
        grads[ga, ky, 0] = cosine[re] + sine[im]
        grads[ga, ky, 1] = cosine[im] - sine[re]
    grads_args = (lambda g: grads.at[ga], lambda g: grads.at[g], gm_send, gm_recv)
    start_across(*grads_args)
    wait_across(*modes_args)
    wait_across(*grads_args)
    for ky in range(2):
        factor = jnp.where(2 * dev + ky == 0, 1.0, 2.0).astype(F32) / (XC * YC)
        for c in range(3):
            out_re, out_im = 0.0, 0.0
            for b in range(GA):
                x_re = modes[b, 8 * ky + 2 * c : 8 * ky + 2 * c + 1, :]
                x_im = modes[b, 8 * ky + 2 * c + 1 : 8 * ky + 2 * c + 2, :]
                g_re, g_im = grads[b, ky, 0], grads[b, ky, 1]
                out_re = out_re + (x_re * g_re + x_im * g_im)
                out_im = out_im + (x_re * g_im - x_im * g_re)
            t_out[ky, 0, c] = out_re * factor
            t_out[ky, 1, c] = out_im * factor
    state_copy.wait()


def expand_kernel(lift_h, t_h, state_h, out_h, new_state_h, lift, t, state, lift_wide, out, sem):
    loads = [
        pltpu.make_async_copy(a, b, sem.at[n]) for n, (a, b) in enumerate(((lift_h, lift), (t_h, t), (state_h, state)))
    ]
    for c in loads:
        c.start()
    forward = pltpu.make_async_copy(state, new_state_h, sem.at[19])
    loads[0].wait()
    for c in range(3):
        lift_wide[c] = widened(lift[...], c)
    loads[1].wait()

    def stretch(n):
        ky, rest = n // 8, n % 8
        part, rows = rest // 4, pl.ds(8 * (rest % 4), 8)
        return pltpu.make_async_copy(out.at[ky, part, rows], out_h.at[ky, part, rows], sem.at[3 + n])

    def body(n, carry):
        ky, rest = n // 8, n % 8
        part, first = rest // 4, 8 * (rest % 4)
        terms = [t[ky, part, c] for c in range(3)]
        for i in range(8):
            total = 0.0
            for c in range(3):
                total = total + jnp.broadcast_to(lift_wide[c, pl.ds(first + i, 1), :], (WIDTH, 128)) * terms[c]
            out[ky, part, first + i] = total
        stretch(n).start()
        return carry

    lax.fori_loop(0, 4, body, 0)
    loads[2].wait()
    forward.start()
    lax.fori_loop(4, 16, body, 0)

    def done(n, carry):
        stretch(n).wait()
        return carry

    lax.fori_loop(0, 16, done, 0)
    forward.wait()


def per_device(consts, density, velocity, pressure, lift, spectral, pointwise, project):
    hbm = pl.BlockSpec(memory_space=pl.ANY)
    V = pltpu.VMEM
    dma = pltpu.SemaphoreType.DMA
    field = V((5, 384, 128), F32)
    rows = V((512, 128), F32)
    coarse = V((GA, 48, 128), F32)
    scratch = [
        V((4, 32, 256), F32), V((3, 4, 32, 256), F32), V((4, 32, 256), F32), V((3, WIDTH), BF16), V((WIDTH, WIDTH), BF16),
        V((3, WIDTH), BF16), V((5, 4, 32, 256), F32), V((3, WIDTH, 128), F32),
        V((2, 2, WIDTH, WIDTH, 128), BF16), V((2, 128, 512), BF16), V((2, 128, 512), BF16), V((2, 512, 128), BF16),
        V((2, 256, 512), BF16), V((2, 512, 256), BF16), V((256, 128), BF16),
        field, field, field, field, field, V((3, 5, 8, 384), F32),
        V((2, 5, 8, 128), F32), V((2, 2, 5, 8, 128), F32), V((2, 5, 8, 128), F32), V((4, 5, 8, 128), F32),
        V((384, 128), F32), coarse, coarse, coarse, coarse, rows, rows, rows, rows, rows, rows,
        V((2, 2, 3, WIDTH, 128), F32), V((GA, 16, 128), F32), V((GA, 2, 2, WIDTH, 128), F32),
        V((128, 512), BF16), V((128, 512), BF16), V((512, 512), F32), V((512, 48), F32),
        V((512, 512), BF16), V((512, 512), BF16), V((4, 128, 128), F32), V((48, 512), F32), V((48, 512), BF16),
        dma((14,)), dma((10,)), dma((10,)), dma((GA,)), dma((GA,)), dma((GA,)), dma((GA,)),
        dma((DEV,)), dma((DEV,)), dma((DEV,)), dma((DEV,)), dma((DEV,)), dma((DEV,)),
        dma((GA,)), dma((GA,)), dma((GA,)), dma((GA,)),
    ]
    new_state, t = pl.pallas_call(
        kernel,
        out_shape=(
            jax.ShapeDtypeStruct((5, 4, 32, 256), F32),
            jax.ShapeDtypeStruct((2, 2, 3, WIDTH, 128), F32),
        ),
        in_specs=[hbm] * 13,
        out_specs=(hbm, pl.BlockSpec(memory_space=pltpu.VMEM)),
        scratch_shapes=scratch,
        compiler_params=pltpu.CompilerParams(
            collective_id=0, has_side_effects=True, vmem_limit_bytes=VMEM_BYTES
        ),
    )(density, velocity, pressure, lift, pointwise, project.T, spectral, *consts)
    grad, new_state = pl.pallas_call(
        expand_kernel,
        out_shape=(
            jax.ShapeDtypeStruct((2, 2, WIDTH, WIDTH, 128), F32),
            jax.ShapeDtypeStruct((5, 4, 32, 256), F32),
        ),
        in_specs=[hbm] * 3,
        out_specs=(hbm, hbm),
        scratch_shapes=[
            V((3, WIDTH), BF16), V((2, 2, 3, WIDTH, 128), F32), V((5, 4, 32, 256), F32), V((3, WIDTH, 128), F32),
            V((2, 2, WIDTH, WIDTH, 128), F32), dma((20,)),
        ],
        compiler_params=pltpu.CompilerParams(vmem_limit_bytes=VMEM_BYTES),
    )(lift, t, new_state)
    return new_state, grad


def solution(mesh):
    in_specs = (
        P(None, "dev", "ga"),
        P(None, None, "dev", "ga"),
        P(None, "dev", "ga"),
        P(),
        P("dev", None, None, None, None),
        P(),
        P(),
    )
    out_specs = (P(None, None, "dev", "ga"), P("dev", None, None, None, None))

    def whole(*args):
        consts = tables()
        return jax.shard_map(
            lambda *a: per_device(a[:6], *a[6:]),
            mesh=mesh, in_specs=(P(),) * 6 + in_specs, out_specs=out_specs, check_vma=False,
        )(*[jnp.asarray(c) for c in consts], *args)

    return whole
```

```python
import functools
import math

import jax
import jax.numpy as jnp
import numpy as np
from jax import lax
from jax.experimental import pallas as pl
from jax.experimental.pallas import tpu as pltpu
from jax.sharding import PartitionSpec as P

MESH = pl.DeviceIdType.MESH
F32 = jnp.float32
BF16 = jnp.bfloat16
WIDTH = 32
MODES = 64
XC = 512
YC = 512
GA = 4
DEV = 32
DT = 0.12
OFFSETS = sorted(
    ((a, b, c) for a in range(4) for b in range(4) for c in range(2) if a + b + c),
    key=lambda o: (-min(o[0], 4 - o[0]) - min(o[1], 4 - o[1]), o),
)
VMEM_BYTES = 62 * 1024 * 1024


def tables():
    def split(a):
        a = np.asarray(a, np.float32)
        hi = a.astype(jnp.bfloat16)
        lo = (a - hi.astype(np.float32)).astype(jnp.bfloat16)
        return np.ascontiguousarray(np.stack([hi, lo]))

    ky = np.arange(MODES)
    y = np.arange(YC)
    ang = 2 * np.pi * ((ky[:, None] * y[None, :]) % YC) / YC
    fwd = np.stack([np.cos(ang), -np.sin(ang)], axis=1)
    weight = np.where(ky == 0, 1.0, 2.0) / (XC * YC)
    inv = fwd * weight[:, None, None]
    fwd_dj = fwd.reshape(DEV, 4, YC)
    fwd_jd = fwd_dj.transpose(1, 0, 2).reshape(128, YC)
    inv_jd = inv.reshape(DEV, 4, YC).transpose(1, 0, 2).reshape(128, YC).T
    q = np.arange(2 * MODES)
    kx = np.where(q < MODES, q, XC - 2 * MODES + q)
    ax = 2 * np.pi * ((kx[:, None] * np.arange(XC)[None, :]) % XC) / XC
    cx = np.concatenate([np.cos(ax), np.sin(ax)], axis=0)
    cx_halves = cx.reshape(256, DEV, 2, 8).transpose(0, 2, 1, 3).reshape(256, XC)
    inv_hi, inv_lo = split(inv_jd)

    pool = np.zeros((256, 128), np.float32)
    pool[np.arange(256), np.arange(256) // 2] = 0.25
    return (
        split(fwd_dj.reshape(128, YC)),
        split(fwd_jd),
        np.concatenate([inv_hi, inv_hi, inv_lo], axis=1),
        split(cx_halves),
        split(cx.T),
        pool.astype(jnp.bfloat16),
    )


def split2(a):
    hi = a.astype(BF16)
    return hi, (a - hi.astype(F32)).astype(BF16)


def nn(a, b):
    return lax.dot_general(a, b, (((1,), (0,)), ((), ())), preferred_element_type=F32)


def nt(a, b):
    return lax.dot_general(a, b, (((1,), (1,)), ((), ())), preferred_element_type=F32)


def tn(a, b):
    return lax.dot_general(a, b, (((0,), (0,)), ((), ())), preferred_element_type=F32)


def primitives(u):
    inv = 1.0 / u[0]
    v = [u[1] * inv, u[2] * inv, u[3] * inv]
    kinetic = u[1] * v[0] + u[2] * v[1] + u[3] * v[2]
    p = 0.4 * (u[4] - 0.5 * kinetic)
    sound = jnp.sqrt(1.4 * p * inv)
    return v, p, sound


def directional(u, v, p, sound, d):
    n = v[d]
    flux = [u[1 + d]]
    for i in range(3):
        f = u[1 + i] * n
        flux.append(f + p if i == d else f)
    flux.append((u[4] + p) * n)
    return flux, jnp.abs(n) + sound


def faces(ul, ur, fl, fr, sl, sr):
    top = jnp.maximum(sl, sr)
    return [(a + b) - top * (d - c) for a, b, c, d in zip(fl, fr, ul, ur)]


def widened(lift, c):
    pick = (lax.broadcasted_iota(jnp.int32, (3, 128), 0) == c).astype(F32).astype(BF16)
    return tn(lift, pick)


def rim_rates(u):
    v, p, sound = primitives(u)
    total, along_y = None, None
    for d, (axis, step, size) in enumerate(((0, 2, 8), (1, 8, 384), (1, 1, 384))):
        flux, speed = directional(u, v, p, sound, d)

        def up(a):
            return pltpu.roll(a, size - step, axis)

        g = faces(u, [up(a) for a in u], flux, [up(a) for a in flux], speed, up(speed))
        div = [a - pltpu.roll(a, step, axis) for a in g]
        total = div if total is None else [a + b for a, b in zip(total, div)]
        along_y = g
    return total, along_y


def block_rates(src, edge, r0):
    lane = lax.broadcasted_iota(jnp.int32, (4, 8, 128), 2)
    odd = lax.broadcasted_iota(jnp.int32, (4, 8, 128), 1) % 2 == 1
    last = lane == 127
    base = pl.multiple_of(8 * (r0 - 1), 8)
    wide = [src[f, pl.ds(base, 48), :].reshape(6, 8, 128) for f in range(5)]
    v, p, sound = primitives(wide)
    flux, speed = directional(wide, v, p, sound, 1)
    g = faces(
        [a[:5] for a in wide], [a[1:] for a in wide], [a[:5] for a in flux], [a[1:] for a in flux], speed[:5], speed[1:]
    )
    total = [a[1:] - a[:4] for a in g]
    u = [a[1:5] for a in wide]
    v = [a[1:5] for a in v]
    p, sound = p[1:5], sound[1:5]

    flux, speed = directional(u, v, p, sound, 0)

    def up_z(a):
        return pltpu.roll(a, 6, 1)

    g = faces(u, [up_z(a) for a in u], flux, [up_z(a) for a in flux], speed, up_z(speed))
    total = [t + (a - pltpu.roll(a, 2, 1)) for t, a in zip(total, g)]

    flux, speed = directional(u, v, p, sound, 2)

    def up_y(a):
        near = pltpu.roll(a, 127, 2)
        return jnp.where(last, pltpu.roll(near, 7, 1), near)

    g = faces(u, [up_y(a) for a in u], flux, [up_y(a) for a in flux], speed, up_y(speed))
    at = pl.multiple_of(8 * r0, 8)
    for f in range(5):
        outer = edge[f, pl.ds(at, 32), :].reshape(4, 8, 128)
        upper = jnp.where(last & odd, outer, g[f])
        wrapped = jnp.where(odd, pltpu.roll(g[f], 1, 1), outer)
        lower = pltpu.roll(jnp.where(last, wrapped, g[f]), 1, 2)
        total[f] = total[f] + (upper - lower)
    return total


def kernel(
    density_h, velocity_h, pressure_h, lift_h, pointwise_h, project_h, spectral_h,
    fdj_h, fjd_h, inv_h, cx_h, cxt_h, pool_h,
    new_state_h, t_out,
    density, velocity, pressure, lift, pointwise, project, new_state, lift_wide,
    spectral, fdj, fjd, inv, cx, cxt, pool,
    u0, ua, ub, acc, edge, rim, own_edge, side_edge, row_edge, corner_edge,
    pooled, snd_in, rcv_in, snd_tg, rcv_tg, snd_x, rcv_x, snd_b, rcv_b, snd_g, rcv_g,
    contracted, modes, grads, rt, slope, made, dp_hi, dp_lo, ft, lpx_ref, pxt_ref,
    load_sem, halo_send, halo_recv, in_send, in_recv, tg_send, tg_recv, x_send, x_recv, b_send, b_recv,
    g_send, g_recv, xm_send, xm_recv, gm_send, gm_recv,
):
    ga = lax.axis_index("ga")
    dev = lax.axis_index("dev")
    east, west = lax.rem(ga + 1, GA), lax.rem(ga + GA - 1, GA)
    south, north = lax.rem(dev + 1, DEV), lax.rem(dev + DEV - 1, DEV)

    loads = [
        pltpu.make_async_copy(a, b, load_sem.at[n])
        for n, (a, b) in enumerate(
            (
                (pool_h, pool), (spectral_h, spectral), (fdj_h, fdj), (cx_h, cx), (cxt_h, cxt), (inv_h, inv), (fjd_h, fjd),
                (density_h, density), (velocity_h, velocity), (pressure_h, pressure),
                (lift_h, lift), (pointwise_h, pointwise), (project_h, project),
            )
        )
    ]
    for n in (7, 8, 9, 0, 10, 11, 12, 1, 2, 3, 4, 5, 6):
        loads[n].start()

    barrier = pltpu.get_barrier_semaphore()

    def greet(s, carry):
        pl.semaphore_signal(barrier, inc=1, device_id=(ga, lax.rem(dev + s, DEV)), device_id_type=MESH)
        return carry

    lax.fori_loop(1, DEV, greet, 0)
    for s in range(1, GA):
        pl.semaphore_signal(barrier, inc=1, device_id=(lax.rem(ga + s, GA), dev), device_id_type=MESH)
    for a in (east, west):
        for b in (south, north):
            pl.semaphore_signal(barrier, inc=1, device_id=(a, b), device_id_type=MESH)

    core, chip_x, chip_y = lax.rem(dev, 2), lax.rem(lax.div(dev, 2), 4), lax.div(dev, 8)

    def exchange_rows(snd, rcv, ssem, rsem, unit):
        for dy, dx, dc in OFFSETS:
            peer = lax.rem(chip_y + dy, 4) * 8 + lax.rem(chip_x + dx, 4) * 2 + lax.rem(core + dc, 2)
            pltpu.make_async_remote_copy(
                src_ref=snd.at[pl.ds(pl.multiple_of(unit * peer, unit), unit)],
                dst_ref=rcv.at[pl.ds(pl.multiple_of(unit * dev, unit), unit)],
                send_sem=ssem.at[peer], recv_sem=rsem.at[dev],
                device_id=(ga, peer), device_id_type=MESH,
            ).start()
        mine = pl.ds(pl.multiple_of(unit * dev, unit), unit)
        rcv[mine, :] = snd[mine, :]

    def wait_rows(snd, rcv, ssem, rsem, unit):
        def go(s, carry):
            peer = lax.rem(dev + s, DEV)
            at = pl.ds(pl.multiple_of(unit * peer, unit), unit)
            pltpu.make_async_remote_copy(
                src_ref=snd.at[at], dst_ref=rcv.at[at], send_sem=ssem.at[peer], recv_sem=rsem.at[peer],
                device_id=(ga, peer), device_id_type=MESH,
            ).wait()
            return carry

        lax.fori_loop(1, DEV, go, 0)

    def across(s, src, dst, ssem, rsem, arriving):
        peer = lax.rem(ga + s, GA)
        return pltpu.make_async_remote_copy(
            src_ref=src(peer), dst_ref=dst(peer if arriving else ga), send_sem=ssem.at[peer],
            recv_sem=rsem.at[peer if arriving else ga], device_id=(peer, dev), device_id_type=MESH,
        )

    def start_across(src, dst, ssem, rsem):
        for s in (2, 1, 3):
            across(s, src, dst, ssem, rsem, False).start()

    def wait_across(src, dst, ssem, rsem):
        for s in (2, 1, 3):
            across(s, src, dst, ssem, rsem, True).wait()

    def coarsen(rows, snd):
        hi, lo = split2(rows)
        pooled[...] = nn(hi, pool[...]) + nn(lo, pool[...])
        both = pooled[pl.ds(0, 192, stride=2), :] + pooled[pl.ds(1, 192, stride=2), :]
        snd[...] = both.reshape(GA, 48, 128)

    for n in (7, 8, 9):
        loads[n].wait()
    for p in range(4):
        for h in range(2):
            cols = slice(128 * h, 128 * h + 128)
            rho = density[p, :, cols]
            v = [velocity[c, p, :, cols] for c in range(3)]
            where = pl.ds(32 + 2 * p + h, 32, stride=8)
            u0[0, where, :] = rho
            for c in range(3):
                u0[1 + c, where, :] = rho * v[c]
            u0[4, where, :] = pressure[p, :, cols] / 0.4 + 0.5 * rho * (v[0] * v[0] + v[1] * v[1] + v[2] * v[2])

    lane1 = lax.broadcasted_iota(jnp.int32, (8, 128), 1)
    for w in range(2):
        for f in range(5):
            packed = None
            for k in range(16):
                row = pltpu.roll(u0[f, pl.ds(8 * (16 * w + k + 4), 8), :], (4 + 8 * k) % 128, 1)
                packed = row if packed is None else jnp.where(lane1 >= 8 * k, row, packed)
            own_edge[w, f] = packed

    loads[0].wait()
    coarsen(jnp.concatenate([velocity[c, p] for p in range(4) for c in range(3)], axis=0), snd_in)

    pl.semaphore_wait(barrier, DEV - 1 + GA - 1 + 4)

    def halo(n, src, dst, target):
        return pltpu.make_async_remote_copy(
            src_ref=src, dst_ref=dst, send_sem=halo_send.at[n], recv_sem=halo_recv.at[n],
            device_id=target, device_id_type=MESH,
        )

    halos = [
        halo(0, u0.at[:, pl.ds(8 * 32, 32)], u0.at[:, pl.ds(0, 32)], (ga, south)),
        halo(1, u0.at[:, pl.ds(8 * 4, 32)], u0.at[:, pl.ds(8 * 36, 32)], (ga, north)),
        halo(2, own_edge.at[1], row_edge.at[0], (ga, south)),
        halo(3, own_edge.at[0], row_edge.at[1], (ga, north)),
        halo(4, own_edge, side_edge.at[0], (east, dev)),
        halo(5, own_edge, side_edge.at[1], (west, dev)),
        halo(6, own_edge.at[1], corner_edge.at[0], (east, south)),
        halo(7, own_edge.at[0], corner_edge.at[1], (east, north)),
        halo(8, own_edge.at[1], corner_edge.at[2], (west, south)),
        halo(9, own_edge.at[0], corner_edge.at[3], (west, north)),
    ]
    in_args = (lambda g: snd_in.at[g], lambda g: rcv_in.at[g], in_send, in_recv)
    start_across(*in_args)
    for c in halos:
        c.start()
    rcv_in[ga] = snd_in[ga]

    for n in (10, 11, 12, 1):
        loads[n].wait()
    for c in range(3):
        lift_wide[c] = widened(lift[...], c)
    for ky in range(2):
        for part in range(2):

            def add(w8, total, ky=ky, part=part):
                total = list(total)
                for n in range(4):
                    w = 4 * w8 + n
                    s = spectral[ky, part, w].astype(F32)
                    for c in range(3):
                        total[c] = total[c] + jnp.broadcast_to(lift_wide[c, pl.ds(w, 1), :], (WIDTH, 128)) * s
                return tuple(total)

            zero = jnp.zeros((WIDTH, 128), F32)
            done = lax.fori_loop(0, WIDTH // 4, add, (zero, zero, zero))
            for c in range(3):
                contracted[ky, part, c] = done[c]

    tile_o = (
        lax.broadcasted_iota(jnp.int32, (WIDTH, 512), 1) % WIDTH == lax.broadcasted_iota(jnp.int32, (WIDTH, 512), 0)
    ).astype(F32).astype(BF16)
    same_row = (
        lax.broadcasted_iota(jnp.int32, (48, 512), 1) // WIDTH == lax.broadcasted_iota(jnp.int32, (48, 512), 0) % 16
    )

    def spread(a):
        return jnp.where(
            same_row, jnp.concatenate([jnp.broadcast_to(a[c : c + 1], (16, 512)) for c in range(3)], axis=0), 0.0
        )

    lp_hi, lp_lo = split2(nn(lift[...], pointwise[...]))
    lpx_ref[...] = spread(nn(lp_hi, tile_o) + nn(lp_lo, tile_o))
    spread_out = jnp.concatenate([spread(nn(project[...], tile_o)), jnp.zeros((80, 512), F32)], axis=0)
    pxt_ref[...] = jnp.concatenate([spread_out, spread_out], axis=0).astype(BF16)

    wait_across(*in_args)
    loads[2].wait()
    hi, lo = split2(jnp.concatenate([rcv_in[g] for g in range(GA)], axis=1))
    freq = nt(hi, fdj[0]) + nt(hi, fdj[1]) + nt(lo, fdj[0])
    for d in range(DEV):
        packed = None
        for n in range(6):
            h, c = n // 3, n % 3
            piece = pltpu.roll(freq[16 * c + 8 * h : 16 * c + 8 * h + 8], (16 * h + 4 * c - 4 * d) % 128, 1)
            packed = piece if packed is None else jnp.where(lane1 >= 16 * h + 4 * c, piece, packed)
        snd_x[pl.ds(8 * d, 8), :] = packed
    x_args = (snd_x, rcv_x, x_send, x_recv, 8)
    exchange_rows(*x_args)

    for c in halos:
        c.wait()
    sub1 = lax.broadcasted_iota(jnp.int32, (8, 128), 0)
    even, first = sub1 % 2 == 0, lane1 % 8 < 4
    low = lane1 < 64
    for f in range(5):
        own = [own_edge[0, f], own_edge[1, f], jnp.where(low, row_edge[1, f], row_edge[0, f])]
        left = [side_edge[0, 0, f], side_edge[0, 1, f], jnp.where(low, corner_edge[1, f], corner_edge[0, f])]
        right = [side_edge[1, 0, f], side_edge[1, 1, f], jnp.where(low, corner_edge[3, f], corner_edge[2, f])]
        for n in range(3):
            rim[0, f, :, 128 * n : 128 * n + 128] = jnp.where(
                even,
                jnp.where(first, pltpu.roll(left[n], 7, 0), own[n]),
                jnp.where(first, own[n], pltpu.roll(right[n], 1, 0)),
            )

    def stage(src, dst, ahead, gain, first_row, blocks, first_stage, rim_src, rim_dst):
        total, along_y = rim_rates([rim[rim_src, f] for f in range(5)])
        for f in range(5):
            if rim_dst is not None:
                rim[rim_dst, f] = rim[0, f] - (0.5 * ahead) * total[f]
            for n in range(3):
                for k in range(16):
                    edge[f, pl.ds(8 * ((16 * n + k + 4) % 48), 8), :] = pltpu.roll(
                        along_y[f][:, 128 * n : 128 * n + 128], 124 - 8 * k, 1
                    )

        def block(n, carry):
            r0 = first_row + 4 * n
            if first_stage:
                r0 = jnp.minimum(r0, 35)
            total = block_rates(src, edge, r0)
            at = pl.ds(pl.multiple_of(8 * r0, 8), 32)
            for f in range(5):
                t = total[f].reshape(32, 128)
                start = u0[f, at, :]
                if dst is not None:
                    dst[f, at, :] = start - (0.5 * ahead) * t
                old = start if first_stage else acc[f, at, :]
                acc[f, at, :] = old - (0.5 * gain) * t
            return carry

        lax.fori_loop(0, blocks, block, 0)

    stage(u0, ua, 0.5 * DT, DT / 6, 1, 10, True, 0, 1)
    stage(ua, ub, 0.5 * DT, DT / 3, 2, 9, False, 1, 2)

    wait_rows(*x_args)
    loads[3].wait()
    hi, lo = split2(rcv_x[...])
    turned = 0.0
    for h in range(2):
        cols = slice(256 * h, 256 * h + 256)
        half = nn(cx[0, :, cols], hi) + nn(cx[1, :, cols], hi) + nn(cx[0, :, cols], lo)
        turned = turned + (pltpu.roll(half, 112, 1) if h else half)
    cosine, sine = turned[:128].T, turned[128:].T
    for ky in range(2):
        for c in range(3):
            r = 4 * c + 2 * ky
            modes[ga, 8 * ky + 2 * c : 8 * ky + 2 * c + 1, :] = cosine[r : r + 1] + sine[r + 1 : r + 2]
            modes[ga, 8 * ky + 2 * c + 1 : 8 * ky + 2 * c + 2, :] = cosine[r + 1 : r + 2] - sine[r : r + 1]
        modes[ga, 8 * ky + 6 : 8 * ky + 8, :] = jnp.zeros((2, 128), F32)
    modes_args = (lambda g: modes.at[ga], lambda g: modes.at[g], xm_send, xm_recv)
    start_across(*modes_args)
    mine = modes[ga]
    rows = []
    for ky in range(2):
        out_re, out_im = 0.0, 0.0
        for c in range(3):
            a = mine[8 * ky + 2 * c : 8 * ky + 2 * c + 1]
            b = mine[8 * ky + 2 * c + 1 : 8 * ky + 2 * c + 2]
            re, im = contracted[ky, 0, c], contracted[ky, 1, c]
            out_re = out_re + (a * re - b * im)
            out_im = out_im + (a * im + b * re)
        rows.append(jnp.concatenate([out_re, -out_im], axis=1))
        rows.append(jnp.concatenate([out_im, out_re], axis=1))
    hi, lo = split2(jnp.concatenate(rows, axis=0))
    loads[4].wait()
    snd_b[...] = nt(cxt[0], hi) + nt(cxt[1], hi) + nt(cxt[0], lo)
    b_args = (snd_b, rcv_b, b_send, b_recv, 16)
    exchange_rows(*b_args)

    stage(ub, ua, DT, DT / 3, 2, 9, False, 2, 1)
    stage(ua, None, DT, DT / 6, 4, 8, False, 1, None)

    after = []
    for p in range(4):
        parts = []
        for h in range(2):
            where = pl.ds(32 + 2 * p + h, 32, stride=8)
            cols = slice(128 * h, 128 * h + 128)
            u = [acc[f, where, :] for f in range(5)]
            for f in range(5):
                new_state[f, p, :, cols] = u[f]
            inv_rho = 1.0 / u[0]
            parts.append([u[1 + c] * inv_rho for c in range(3)])
        for c in range(3):
            after.append(jnp.concatenate([parts[0][c], parts[1][c]], axis=1))
    coarsen(jnp.concatenate(after, axis=0), snd_tg)
    state_copy = pltpu.make_async_copy(new_state, new_state_h, load_sem.at[13])
    state_copy.start()
    tg_args = (lambda g: snd_tg.at[g], lambda g: rcv_tg.at[g], tg_send, tg_recv)
    start_across(*tg_args)
    rcv_tg[ga] = snd_tg[ga]

    lpx_hi, lpx_lo = split2(lpx_ref[...])

    def transposed(a):
        return jnp.concatenate([a, jnp.zeros((80, 128), F32)], axis=0).T

    for g in range(GA):
        ins_hi, ins_lo = split2(transposed(rcv_in[g])[:, :48])
        slope[pl.ds(128 * g, 128), :] = nn(ins_hi, lpx_hi) + nn(ins_hi, lpx_lo) + nn(ins_lo, lpx_hi)

    wait_rows(*b_args)
    loads[5].wait()
    group = lax.broadcasted_iota(jnp.int32, (32, 128), 1) // 32
    for t in range(4):
        src = [rcv_b[pl.ds(4 * t + m, 32, stride=16), :] for m in range(4)]
        for j in range(4):
            made_of = None
            for m in range(4):
                turn = (32 * (m - j)) % 128
                piece = pltpu.roll(src[m], turn, 1) if turn else src[m]
                made_of = piece if made_of is None else jnp.where(group == m, piece, made_of)
            hi, lo = split2(made_of)
            for n, piece in enumerate((hi, lo, hi)):
                rt[pl.ds(128 * n + 32 * j, 32), 128 * t : 128 * t + 128] = piece

    k0, k1 = math.sqrt(2.0 / math.pi), 0.044715

    def forward(g, carry):
        at = pl.ds(pl.multiple_of(128 * g, 128), 128)
        pre = slope[at, :] + nn(inv[at, :], rt[...])
        square = pre * pre
        t = jnp.tanh(k0 * pre * (1.0 + k1 * square))
        half = 0.5 * (1.0 + t)
        slope[at, :] = half + (0.5 * k0) * pre * (1.0 - t * t) * (1.0 + (3.0 * k1) * square)
        hi, lo = split2(pre * half)
        made[at, :] = nt(hi, pxt_ref[:128]) + nt(lo, pxt_ref[:128])
        return carry

    lax.fori_loop(0, GA, forward, 0)

    wait_across(*tg_args)

    def backward(g, carry):
        at = pl.ds(pl.multiple_of(128 * g, 128), 128)
        hi, lo = split2(made[at, :] - transposed(rcv_tg[g]))
        d_pre = nn(jnp.concatenate([hi, lo], axis=1), pxt_ref[...]) * slope[at, :]
        hi, lo = split2(d_pre)
        dp_hi[at, :] = hi
        dp_lo[at, :] = lo
        return carry

    lax.fori_loop(0, GA, backward, 0)
    loads[6].wait()
    for t in range(2):
        cols = slice(256 * t, 256 * t + 256)
        both = nn(fjd[0], dp_hi[:, cols]) + nn(fjd[1], dp_hi[:, cols]) + nn(fjd[0], dp_lo[:, cols])
        ft[2 * t], ft[2 * t + 1] = both[:, :128], both[:, 128:]
    for t in range(4):
        src = [ft[t, pl.ds(32 * j, 32), :] for j in range(4)]
        for m in range(4):
            made_of = None
            for j in range(4):
                turn = (32 * (j - m)) % 128
                piece = pltpu.roll(src[j], turn, 1) if turn else src[j]
                made_of = piece if made_of is None else jnp.where(group == j, piece, made_of)
            snd_g[pl.ds(4 * t + m, 32, stride=16), :] = made_of
    g_args = (snd_g, rcv_g, g_send, g_recv, 16)
    exchange_rows(*g_args)
    wait_rows(*g_args)

    arrived = rcv_g[...].reshape(DEV, 2, 8, 128)
    hi, lo = split2(jnp.concatenate([arrived[:, h].reshape(256, 128) for h in range(2)], axis=0))
    turned = nn(cx[0], hi) + nn(cx[1], hi) + nn(cx[0], lo)
    cosine, sine = turned[:128].T, turned[128:].T
    for ky in range(2):
        re, im = slice(64 * ky, 64 * ky + 32), slice(64 * ky + 32, 64 * ky + 64)
        grads[ga, ky, 0] = cosine[re] + sine[im]
        grads[ga, ky, 1] = cosine[im] - sine[re]
    grads_args = (lambda g: grads.at[ga], lambda g: grads.at[g], gm_send, gm_recv)
    start_across(*grads_args)
    wait_across(*modes_args)
    wait_across(*grads_args)
    for ky in range(2):
        factor = jnp.where(2 * dev + ky == 0, 1.0, 2.0).astype(F32) / (XC * YC)
        for c in range(3):
            out_re, out_im = 0.0, 0.0
            for b in range(GA):
                x_re = modes[b, 8 * ky + 2 * c : 8 * ky + 2 * c + 1, :]
                x_im = modes[b, 8 * ky + 2 * c + 1 : 8 * ky + 2 * c + 2, :]
                g_re, g_im = grads[b, ky, 0], grads[b, ky, 1]
                out_re = out_re + (x_re * g_re + x_im * g_im)
                out_im = out_im + (x_re * g_im - x_im * g_re)
            t_out[ky, 0, c] = out_re * factor
            t_out[ky, 1, c] = out_im * factor
    state_copy.wait()


def expand_kernel(lift_h, t_h, state_h, out_h, new_state_h, lift, t, state, lift_wide, out, sem):
    loads = [
        pltpu.make_async_copy(a, b, sem.at[n]) for n, (a, b) in enumerate(((lift_h, lift), (t_h, t), (state_h, state)))
    ]
    for c in loads:
        c.start()
    forward = pltpu.make_async_copy(state, new_state_h, sem.at[19])
    loads[0].wait()
    for c in range(3):
        lift_wide[c] = widened(lift[...], c)
    loads[1].wait()

    def stretch(n):
        ky, rest = n // 8, n % 8
        part, rows = rest // 4, pl.ds(8 * (rest % 4), 8)
        return pltpu.make_async_copy(out.at[ky, part, rows], out_h.at[ky, part, rows], sem.at[3 + n])

    def body(n, carry):
        ky, rest = n // 8, n % 8
        part, first = rest // 4, 8 * (rest % 4)
        terms = [t[ky, part, c] for c in range(3)]
        for i in range(8):
            total = 0.0
            for c in range(3):
                total = total + jnp.broadcast_to(lift_wide[c, pl.ds(first + i, 1), :], (WIDTH, 128)) * terms[c]
            out[ky, part, first + i] = total
        stretch(n).start()
        return carry

    lax.fori_loop(0, 4, body, 0)
    loads[2].wait()
    forward.start()
    lax.fori_loop(4, 16, body, 0)

    def done(n, carry):
        stretch(n).wait()
        return carry

    lax.fori_loop(0, 16, done, 0)
    forward.wait()


def per_device(consts, density, velocity, pressure, lift, spectral, pointwise, project):
    hbm = pl.BlockSpec(memory_space=pl.ANY)
    V = pltpu.VMEM
    dma = pltpu.SemaphoreType.DMA
    field = V((5, 384, 128), F32)
    rows = V((512, 128), F32)
    coarse = V((GA, 48, 128), F32)
    scratch = [
        V((4, 32, 256), F32), V((3, 4, 32, 256), F32), V((4, 32, 256), F32), V((3, WIDTH), BF16), V((WIDTH, WIDTH), BF16),
        V((3, WIDTH), BF16), V((5, 4, 32, 256), F32), V((3, WIDTH, 128), F32),
        V((2, 2, WIDTH, WIDTH, 128), BF16), V((2, 128, 512), BF16), V((2, 128, 512), BF16), V((512, 384), BF16),
        V((2, 256, 512), BF16), V((2, 512, 256), BF16), V((256, 128), BF16),
        field, field, field, field, field, V((3, 5, 8, 384), F32),
        V((2, 5, 8, 128), F32), V((2, 2, 5, 8, 128), F32), V((2, 5, 8, 128), F32), V((4, 5, 8, 128), F32),
        V((384, 128), F32), coarse, coarse, coarse, coarse, V((256, 128), F32), V((256, 128), F32), rows, rows, rows, rows,
        V((2, 2, 3, WIDTH, 128), F32), V((GA, 16, 128), F32), V((GA, 2, 2, WIDTH, 128), F32),
        V((384, 512), BF16), V((512, 512), F32), V((512, 128), F32),
        V((512, 512), BF16), V((512, 512), BF16), V((4, 128, 128), F32), V((48, 512), F32), V((256, 512), BF16),
        dma((14,)), dma((10,)), dma((10,)), dma((GA,)), dma((GA,)), dma((GA,)), dma((GA,)),
        dma((DEV,)), dma((DEV,)), dma((DEV,)), dma((DEV,)), dma((DEV,)), dma((DEV,)),
        dma((GA,)), dma((GA,)), dma((GA,)), dma((GA,)),
    ]
    new_state, t = pl.pallas_call(
        kernel,
        out_shape=(
            jax.ShapeDtypeStruct((5, 4, 32, 256), F32),
            jax.ShapeDtypeStruct((2, 2, 3, WIDTH, 128), F32),
        ),
        in_specs=[hbm] * 13,
        out_specs=(hbm, pl.BlockSpec(memory_space=pltpu.VMEM)),
        scratch_shapes=scratch,
        compiler_params=pltpu.CompilerParams(
            collective_id=0, has_side_effects=True, vmem_limit_bytes=VMEM_BYTES
        ),
    )(density, velocity, pressure, lift, pointwise, project.T, spectral, *consts)
    grad, new_state = pl.pallas_call(
        expand_kernel,
        out_shape=(
            jax.ShapeDtypeStruct((2, 2, WIDTH, WIDTH, 128), F32),
            jax.ShapeDtypeStruct((5, 4, 32, 256), F32),
        ),
        in_specs=[hbm] * 3,
        out_specs=(hbm, hbm),
        scratch_shapes=[
            V((3, WIDTH), BF16), V((2, 2, 3, WIDTH, 128), F32), V((5, 4, 32, 256), F32), V((3, WIDTH, 128), F32),
            V((2, 2, WIDTH, WIDTH, 128), F32), dma((20,)),
        ],
        compiler_params=pltpu.CompilerParams(vmem_limit_bytes=VMEM_BYTES),
    )(lift, t, new_state)
    return new_state, grad


def solution(mesh):
    in_specs = (
        P(None, "dev", "ga"),
        P(None, None, "dev", "ga"),
        P(None, "dev", "ga"),
        P(),
        P("dev", None, None, None, None),
        P(),
        P(),
    )
    out_specs = (P(None, None, "dev", "ga"), P("dev", None, None, None, None))

    def whole(*args):
        consts = tables()
        return jax.shard_map(
            lambda *a: per_device(a[:6], *a[6:]),
            mesh=mesh, in_specs=(P(),) * 6 + in_specs, out_specs=out_specs, check_vma=False,
        )(*[jnp.asarray(c) for c in consts], *args)

    return whole
```

```python
import functools
import math

import jax
import jax.numpy as jnp
import numpy as np
from jax import lax
from jax.experimental import pallas as pl
from jax.experimental.pallas import tpu as pltpu
from jax.sharding import PartitionSpec as P

MESH = pl.DeviceIdType.MESH
F32 = jnp.float32
BF16 = jnp.bfloat16
WIDTH = 32
MODES = 64
XC = 512
YC = 512
GA = 4
DEV = 32
DT = 0.12
BLOCK = 8
OFFSETS = sorted(
    ((a, b, c) for a in range(4) for b in range(4) for c in range(2) if a + b + c),
    key=lambda o: (-min(o[0], 4 - o[0]) - min(o[1], 4 - o[1]), o),
)
VMEM_BYTES = 62 * 1024 * 1024


def tables():
    def split(a):
        a = np.asarray(a, np.float32)
        hi = a.astype(jnp.bfloat16)
        lo = (a - hi.astype(np.float32)).astype(jnp.bfloat16)
        return np.ascontiguousarray(np.stack([hi, lo]))

    ky = np.arange(MODES)
    y = np.arange(YC)
    ang = 2 * np.pi * ((ky[:, None] * y[None, :]) % YC) / YC
    fwd = np.stack([np.cos(ang), -np.sin(ang)], axis=1)
    weight = np.where(ky == 0, 1.0, 2.0) / (XC * YC)
    inv = fwd * weight[:, None, None]
    fwd_dj = fwd.reshape(DEV, 4, YC)
    fwd_jd = fwd_dj.transpose(1, 0, 2).reshape(128, YC)
    inv_jd = inv.reshape(DEV, 4, YC).transpose(1, 0, 2).reshape(128, YC).T
    q = np.arange(2 * MODES)
    kx = np.where(q < MODES, q, XC - 2 * MODES + q)
    ax = 2 * np.pi * ((kx[:, None] * np.arange(XC)[None, :]) % XC) / XC
    cx = np.concatenate([np.cos(ax), np.sin(ax)], axis=0)
    cx_halves = cx.reshape(256, DEV, 2, 8).transpose(0, 2, 1, 3).reshape(256, XC)
    inv_hi, inv_lo = split(inv_jd)

    pool = np.zeros((256, 128), np.float32)
    pool[np.arange(256), np.arange(256) // 2] = 0.25
    return (
        split(fwd_dj.reshape(128, YC)),
        split(fwd_jd),
        np.concatenate([inv_hi, inv_hi, inv_lo], axis=1),
        split(cx_halves),
        split(cx.T),
        pool.astype(jnp.bfloat16),
    )


def split2(a):
    hi = a.astype(BF16)
    return hi, (a - hi.astype(F32)).astype(BF16)


def nn(a, b):
    return lax.dot_general(a, b, (((1,), (0,)), ((), ())), preferred_element_type=F32)


def nt(a, b):
    return lax.dot_general(a, b, (((1,), (1,)), ((), ())), preferred_element_type=F32)


def tn(a, b):
    return lax.dot_general(a, b, (((0,), (0,)), ((), ())), preferred_element_type=F32)


def primitives(u):
    inv = 1.0 / u[0]
    v = [u[1] * inv, u[2] * inv, u[3] * inv]
    kinetic = u[1] * v[0] + u[2] * v[1] + u[3] * v[2]
    p = 0.4 * (u[4] - 0.5 * kinetic)
    sound = jnp.sqrt(1.4 * p * inv)
    return v, p, sound


def directional(u, v, p, sound, d):
    n = v[d]
    flux = [u[1 + d]]
    for i in range(3):
        f = u[1 + i] * n
        flux.append(f + p if i == d else f)
    flux.append((u[4] + p) * n)
    return flux, jnp.abs(n) + sound


def faces(ul, ur, fl, fr, sl, sr):
    top = jnp.maximum(sl, sr)
    return [(a + b) - top * (d - c) for a, b, c, d in zip(fl, fr, ul, ur)]


def widened(lift, c):
    pick = (lax.broadcasted_iota(jnp.int32, (3, 128), 0) == c).astype(F32).astype(BF16)
    return tn(lift, pick)


def rim_rates(u):
    v, p, sound = primitives(u)
    total, along_y = None, None
    for d, (axis, step, size) in enumerate(((0, 2, 8), (1, 8, 384), (1, 1, 384))):
        flux, speed = directional(u, v, p, sound, d)

        def up(a):
            return pltpu.roll(a, size - step, axis)

        g = faces(u, [up(a) for a in u], flux, [up(a) for a in flux], speed, up(speed))
        div = [a - pltpu.roll(a, step, axis) for a in g]
        total = div if total is None else [a + b for a, b in zip(total, div)]
        along_y = g
    return total, along_y


def block_rates(src, edge, r0):
    lane = lax.broadcasted_iota(jnp.int32, (BLOCK, 8, 128), 2)
    odd = lax.broadcasted_iota(jnp.int32, (BLOCK, 8, 128), 1) % 2 == 1
    last = lane == 127
    base = pl.multiple_of(8 * (r0 - 1), 8)
    wide = [src[f, pl.ds(base, 8 * BLOCK + 16), :].reshape(BLOCK + 2, 8, 128) for f in range(5)]
    v, p, sound = primitives(wide)
    flux, speed = directional(wide, v, p, sound, 1)
    g = faces(
        [a[:-1] for a in wide], [a[1:] for a in wide], [a[:-1] for a in flux], [a[1:] for a in flux], speed[:-1], speed[1:]
    )
    total = [a[1:] - a[:-1] for a in g]
    u = [a[1:-1] for a in wide]
    v = [a[1:-1] for a in v]
    p, sound = p[1:-1], sound[1:-1]

    flux, speed = directional(u, v, p, sound, 0)

    def up_z(a):
        return pltpu.roll(a, 6, 1)

    g = faces(u, [up_z(a) for a in u], flux, [up_z(a) for a in flux], speed, up_z(speed))
    total = [t + (a - pltpu.roll(a, 2, 1)) for t, a in zip(total, g)]

    flux, speed = directional(u, v, p, sound, 2)

    def up_y(a):
        near = pltpu.roll(a, 127, 2)
        return jnp.where(last, pltpu.roll(near, 7, 1), near)

    g = faces(u, [up_y(a) for a in u], flux, [up_y(a) for a in flux], speed, up_y(speed))
    at = pl.multiple_of(8 * r0, 8)
    for f in range(5):
        outer = edge[f, pl.ds(at, 8 * BLOCK), :].reshape(BLOCK, 8, 128)
        upper = jnp.where(last & odd, outer, g[f])
        wrapped = jnp.where(odd, pltpu.roll(g[f], 1, 1), outer)
        lower = pltpu.roll(jnp.where(last, wrapped, g[f]), 1, 2)
        total[f] = total[f] + (upper - lower)
    return total


def kernel(
    density_h, velocity_h, pressure_h, lift_h, pointwise_h, project_h, spectral_h,
    fdj_h, fjd_h, inv_h, cx_h, cxt_h, pool_h,
    new_state_h, t_out,
    density, velocity, pressure, lift, pointwise, project, new_state, lift_wide,
    spectral, fdj, fjd, inv, cx, cxt, pool,
    u0, ua, ub, uc, acc, edge, rim, own_edge, side_edge, row_edge, corner_edge,
    pooled, snd_in, rcv_in, snd_tg, rcv_tg, snd_x, rcv_x, snd_b, rcv_b, snd_g, rcv_g,
    contracted, modes, grads, rt, slope, made, dp_hi, dp_lo, ft, lpx_ref, pxt_ref,
    load_sem, halo_send, halo_recv, in_send, in_recv, tg_send, tg_recv, x_send, x_recv, b_send, b_recv,
    g_send, g_recv, relay, xm_send, xm_recv, gm_send, gm_recv,
):
    ga = lax.axis_index("ga")
    dev = lax.axis_index("dev")
    east, west = lax.rem(ga + 1, GA), lax.rem(ga + GA - 1, GA)
    south, north = lax.rem(dev + 1, DEV), lax.rem(dev + DEV - 1, DEV)

    loads = [
        pltpu.make_async_copy(a, b, load_sem.at[n])
        for n, (a, b) in enumerate(
            (
                (pool_h, pool), (spectral_h, spectral), (fdj_h, fdj), (cx_h, cx), (cxt_h, cxt), (inv_h, inv), (fjd_h, fjd),
                (density_h, density), (velocity_h, velocity), (pressure_h, pressure),
                (lift_h, lift), (pointwise_h, pointwise), (project_h, project),
            )
        )
    ]
    for n in (7, 8, 9, 0, 10, 11, 12, 1, 2, 3, 4, 5, 6):
        loads[n].start()

    barrier = pltpu.get_barrier_semaphore()

    core, chip_x, chip_y = lax.rem(dev, 2), lax.rem(lax.div(dev, 2), 4), lax.div(dev, 8)

    def at(dy, dx, dc):
        return lax.rem(chip_y + dy, 4) * 8 + lax.rem(chip_x + dx, 4) * 2 + lax.rem(core + dc, 2)

    beside = jnp.where(core == 1, south, north)
    line_x = [(ga, at(0, k, 0)) for k in range(1, 4)]
    first = [(lax.rem(ga + k, GA), dev) for k in range(1, GA)]
    first += [(ga, at(a, 0, c)) for a in range(4) for c in range(2) if a + c] + line_x + [(ga, beside)]
    for who in first:
        pl.semaphore_signal(barrier, inc=1, device_id=who, device_id_type=MESH)

    def exchange_rows(snd, rcv, ssem, rsem, unit):
        for dy, dx, dc in OFFSETS:
            peer = at(dy, dx, dc)
            pltpu.make_async_remote_copy(
                src_ref=snd.at[pl.ds(pl.multiple_of(unit * peer, unit), unit)],
                dst_ref=rcv.at[pl.ds(pl.multiple_of(unit * dev, unit), unit)],
                send_sem=ssem.at[0], recv_sem=rsem.at[0],
                device_id=(ga, peer), device_id_type=MESH,
            ).start()
        mine = pl.ds(pl.multiple_of(unit * dev, unit), unit)
        rcv[mine, :] = snd[mine, :]

    def wait_rows(snd, rcv, ssem, rsem, unit):
        whole = pl.ds(0, unit * (DEV - 1))
        pltpu.make_async_remote_copy(
            src_ref=snd.at[whole], dst_ref=rcv.at[whole], send_sem=ssem.at[0], recv_sem=rsem.at[0],
            device_id=(ga, south), device_id_type=MESH,
        ).wait()

    def start_across(src, dst, ssem, rsem):
        for k in (2, 1, 3):
            peer = lax.rem(ga + k, GA)
            pltpu.make_async_remote_copy(
                src_ref=src(peer), dst_ref=dst.at[ga], send_sem=ssem.at[0], recv_sem=rsem.at[0],
                device_id=(peer, dev), device_id_type=MESH,
            ).start()

    def wait_across(src, dst, ssem, rsem):
        three = dst.at[pl.ds(0, GA - 1)]
        pltpu.make_async_remote_copy(
            src_ref=three, dst_ref=three, send_sem=ssem.at[0], recv_sem=rsem.at[0],
            device_id=(east, dev), device_id_type=MESH,
        ).wait()

    def coarsen(rows, snd):
        hi, lo = split2(rows)
        pooled[...] = nn(hi, pool[...]) + nn(lo, pool[...])
        both = pooled[pl.ds(0, 192, stride=2), :] + pooled[pl.ds(1, 192, stride=2), :]
        snd[...] = both.reshape(GA, 48, 128)

    for n in (7, 8, 9):
        loads[n].wait()
    for p in range(4):
        for h in range(2):
            cols = slice(128 * h, 128 * h + 128)
            rho = density[p, :, cols]
            v = [velocity[c, p, :, cols] for c in range(3)]
            where = pl.ds(32 + 2 * p + h, 32, stride=8)
            u0[0, where, :] = rho
            for c in range(3):
                u0[1 + c, where, :] = rho * v[c]
            u0[4, where, :] = pressure[p, :, cols] / 0.4 + 0.5 * rho * (v[0] * v[0] + v[1] * v[1] + v[2] * v[2])

    lane1 = lax.broadcasted_iota(jnp.int32, (8, 128), 1)
    for w in range(2):
        for f in range(5):
            packed = None
            for k in range(16):
                row = pltpu.roll(u0[f, pl.ds(8 * (16 * w + k + 4), 8), :], (4 + 8 * k) % 128, 1)
                packed = row if packed is None else jnp.where(lane1 >= 8 * k, row, packed)
            own_edge[w, f] = packed

    loads[0].wait()
    coarsen(jnp.concatenate([velocity[c, p] for p in range(4) for c in range(3)], axis=0), snd_in)

    pl.semaphore_wait(barrier, len(first))
    second = line_x + [(east, dev), (west, dev)]
    for who in second:
        pl.semaphore_signal(relay, inc=1, device_id=who, device_id_type=MESH)

    def halo(n, src, dst, target):
        return pltpu.make_async_remote_copy(
            src_ref=src, dst_ref=dst, send_sem=halo_send.at[n], recv_sem=halo_recv.at[n],
            device_id=target, device_id_type=MESH,
        )

    halos = [
        halo(0, u0.at[:, pl.ds(8 * 32, 32)], u0.at[:, pl.ds(0, 32)], (ga, south)),
        halo(0, u0.at[:, pl.ds(8 * 4, 32)], u0.at[:, pl.ds(8 * 36, 32)], (ga, north)),
        halo(2, own_edge, side_edge.at[0], (east, dev)),
        halo(2, own_edge, side_edge.at[1], (west, dev)),
        halo(1, own_edge.at[1], row_edge.at[0], (ga, south)),
        halo(1, own_edge.at[0], row_edge.at[1], (ga, north)),
    ]
    corners = [
        halo(3, own_edge.at[1], corner_edge.at[0], (east, south)),
        halo(3, own_edge.at[0], corner_edge.at[1], (east, north)),
        halo(3, own_edge.at[1], corner_edge.at[2], (west, south)),
        halo(3, own_edge.at[0], corner_edge.at[3], (west, north)),
    ]
    halo_waits = [
        halo(n, a, a, (ga, south)) for n, a in enumerate((u0.at[:, pl.ds(0, 64)], row_edge, side_edge, corner_edge))
    ]
    in_args = (lambda g: snd_in.at[g], rcv_in, in_send, in_recv)
    start_across(*in_args)
    for c in halos:
        c.start()
    rcv_in[ga] = snd_in[ga]

    for n in (10, 11, 12, 1):
        loads[n].wait()
    for c in range(3):
        lift_wide[c] = widened(lift[...], c)
    for ky in range(2):
        for part in range(2):

            def add(w8, total, ky=ky, part=part):
                total = list(total)
                for n in range(4):
                    w = 4 * w8 + n
                    s = spectral[ky, part, w].astype(F32)
                    for c in range(3):
                        total[c] = total[c] + jnp.broadcast_to(lift_wide[c, pl.ds(w, 1), :], (WIDTH, 128)) * s
                return tuple(total)

            zero = jnp.zeros((WIDTH, 128), F32)
            done = lax.fori_loop(0, WIDTH // 4, add, (zero, zero, zero))
            for c in range(3):
                contracted[ky, part, c] = done[c]

    tile_o = (
        lax.broadcasted_iota(jnp.int32, (WIDTH, 512), 1) % WIDTH == lax.broadcasted_iota(jnp.int32, (WIDTH, 512), 0)
    ).astype(F32).astype(BF16)
    same_row = (
        lax.broadcasted_iota(jnp.int32, (48, 512), 1) // WIDTH == lax.broadcasted_iota(jnp.int32, (48, 512), 0) % 16
    )

    def spread(a):
        return jnp.where(
            same_row, jnp.concatenate([jnp.broadcast_to(a[c : c + 1], (16, 512)) for c in range(3)], axis=0), 0.0
        )

    lp_hi, lp_lo = split2(nn(lift[...], pointwise[...]))
    lpx_ref[...] = spread(nn(lp_hi, tile_o) + nn(lp_lo, tile_o))
    spread_out = jnp.concatenate([spread(nn(project[...], tile_o)), jnp.zeros((80, 512), F32)], axis=0)
    pxt_ref[...] = jnp.concatenate([spread_out, spread_out], axis=0).astype(BF16)

    pl.semaphore_wait(relay, len(second))
    for c in corners:
        c.start()

    wait_across(*in_args)
    loads[2].wait()
    hi, lo = split2(jnp.concatenate([rcv_in[g] for g in range(GA)], axis=1))
    freq = nt(hi, fdj[0]) + nt(hi, fdj[1]) + nt(lo, fdj[0])
    for d in range(DEV):
        packed = None
        for n in range(6):
            h, c = n // 3, n % 3
            piece = pltpu.roll(freq[16 * c + 8 * h : 16 * c + 8 * h + 8], (16 * h + 4 * c - 4 * d) % 128, 1)
            packed = piece if packed is None else jnp.where(lane1 >= 16 * h + 4 * c, piece, packed)
        snd_x[pl.ds(8 * d, 8), :] = packed
    x_args = (snd_x, rcv_x, x_send, x_recv, 8)
    exchange_rows(*x_args)

    for c in halo_waits:
        c.wait()
    sub1 = lax.broadcasted_iota(jnp.int32, (8, 128), 0)
    even, outside = sub1 % 2 == 0, lane1 % 8 < 4
    low = lane1 < 64
    for f in range(5):
        own = [own_edge[0, f], own_edge[1, f], jnp.where(low, row_edge[1, f], row_edge[0, f])]
        left = [side_edge[0, 0, f], side_edge[0, 1, f], jnp.where(low, corner_edge[1, f], corner_edge[0, f])]
        right = [side_edge[1, 0, f], side_edge[1, 1, f], jnp.where(low, corner_edge[3, f], corner_edge[2, f])]
        for n in range(3):
            rim[0, f, :, 128 * n : 128 * n + 128] = jnp.where(
                even,
                jnp.where(outside, pltpu.roll(left[n], 7, 0), own[n]),
                jnp.where(outside, own[n], pltpu.roll(right[n], 1, 0)),
            )

    def stage(src, dst, ahead, first_row, last_row, rim_src, rim_dst):
        total, along_y = rim_rates([rim[rim_src, f] for f in range(5)])
        for f in range(5):
            if rim_dst is not None:
                rim[rim_dst, f] = rim[0, f] - (0.5 * ahead) * total[f]
            for n in range(3):
                for k in range(16):
                    edge[f, pl.ds(8 * ((16 * n + k + 4) % 48), 8), :] = pltpu.roll(
                        along_y[f][:, 128 * n : 128 * n + 128], 124 - 8 * k, 1
                    )

        def block(n, carry):
            r0 = jnp.minimum(first_row + BLOCK * n, last_row + 1 - BLOCK)
            total = block_rates(src, edge, r0)
            at = pl.ds(pl.multiple_of(8 * r0, 8), 8 * BLOCK)
            for f in range(5):
                t = total[f].reshape(8 * BLOCK, 128)
                if dst is not None:
                    dst[f, at, :] = u0[f, at, :] - (0.5 * ahead) * t
                else:
                    mean = (ua[f, at, :] + 2.0 * ub[f, at, :] + uc[f, at, :] - u0[f, at, :]) * (1.0 / 3.0)
                    acc[f, at, :] = mean - (DT / 12.0) * t
            return carry

        lax.fori_loop(0, -(-(last_row + 1 - first_row) // BLOCK), block, 0)

    stage(u0, ua, 0.5 * DT, 1, 38, 0, 1)

    wait_rows(*x_args)
    loads[3].wait()
    hi, lo = split2(rcv_x[...])
    turned = 0.0
    for h in range(2):
        cols = slice(256 * h, 256 * h + 256)
        half = nn(cx[0, :, cols], hi) + nn(cx[1, :, cols], hi) + nn(cx[0, :, cols], lo)
        turned = turned + (pltpu.roll(half, 112, 1) if h else half)
    cosine, sine = turned[:128].T, turned[128:].T
    for ky in range(2):
        for c in range(3):
            r = 4 * c + 2 * ky
            modes[ga, 8 * ky + 2 * c : 8 * ky + 2 * c + 1, :] = cosine[r : r + 1] + sine[r + 1 : r + 2]
            modes[ga, 8 * ky + 2 * c + 1 : 8 * ky + 2 * c + 2, :] = cosine[r + 1 : r + 2] - sine[r : r + 1]
        modes[ga, 8 * ky + 6 : 8 * ky + 8, :] = jnp.zeros((2, 128), F32)
    modes_args = (lambda g: modes.at[ga], modes, xm_send, xm_recv)
    start_across(*modes_args)
    mine = modes[ga]
    rows = []
    for ky in range(2):
        out_re, out_im = 0.0, 0.0
        for c in range(3):
            a = mine[8 * ky + 2 * c : 8 * ky + 2 * c + 1]
            b = mine[8 * ky + 2 * c + 1 : 8 * ky + 2 * c + 2]
            re, im = contracted[ky, 0, c], contracted[ky, 1, c]
            out_re = out_re + (a * re - b * im)
            out_im = out_im + (a * im + b * re)
        rows.append(jnp.concatenate([out_re, -out_im], axis=1))
        rows.append(jnp.concatenate([out_im, out_re], axis=1))
    hi, lo = split2(jnp.concatenate(rows, axis=0))
    loads[4].wait()
    snd_b[...] = nt(cxt[0], hi) + nt(cxt[1], hi) + nt(cxt[0], lo)
    b_args = (snd_b, rcv_b, b_send, b_recv, 16)
    exchange_rows(*b_args)

    stage(ua, ub, 0.5 * DT, 2, 37, 1, 2)
    stage(ub, uc, DT, 3, 36, 2, 1)
    stage(uc, None, DT, 4, 35, 1, None)

    after = []
    for p in range(4):
        parts = []
        for h in range(2):
            where = pl.ds(32 + 2 * p + h, 32, stride=8)
            cols = slice(128 * h, 128 * h + 128)
            u = [acc[f, where, :] for f in range(5)]
            for f in range(5):
                new_state[f, p, :, cols] = u[f]
            inv_rho = 1.0 / u[0]
            parts.append([u[1 + c] * inv_rho for c in range(3)])
        for c in range(3):
            after.append(jnp.concatenate([parts[0][c], parts[1][c]], axis=1))
    coarsen(jnp.concatenate(after, axis=0), snd_tg)
    state_copy = pltpu.make_async_copy(new_state, new_state_h, load_sem.at[13])
    state_copy.start()
    tg_args = (lambda g: snd_tg.at[g], rcv_tg, tg_send, tg_recv)
    start_across(*tg_args)
    rcv_tg[ga] = snd_tg[ga]

    lpx_hi, lpx_lo = split2(lpx_ref[...])

    def transposed(a):
        return jnp.concatenate([a, jnp.zeros((80, 128), F32)], axis=0).T

    for g in range(GA):
        ins_hi, ins_lo = split2(transposed(rcv_in[g])[:, :48])
        slope[pl.ds(128 * g, 128), :] = nn(ins_hi, lpx_hi) + nn(ins_hi, lpx_lo) + nn(ins_lo, lpx_hi)

    wait_rows(*b_args)
    loads[5].wait()
    group = lax.broadcasted_iota(jnp.int32, (32, 128), 1) // 32
    for t in range(4):
        src = [rcv_b[pl.ds(4 * t + m, 32, stride=16), :] for m in range(4)]
        for j in range(4):
            made_of = None
            for m in range(4):
                turn = (32 * (m - j)) % 128
                piece = pltpu.roll(src[m], turn, 1) if turn else src[m]
                made_of = piece if made_of is None else jnp.where(group == m, piece, made_of)
            hi, lo = split2(made_of)
            for n, piece in enumerate((hi, lo, hi)):
                rt[pl.ds(128 * n + 32 * j, 32), 128 * t : 128 * t + 128] = piece

    k0, k1 = math.sqrt(2.0 / math.pi), 0.044715

    def forward(g, carry):
        at = pl.ds(pl.multiple_of(128 * g, 128), 128)
        pre = slope[at, :] + nn(inv[at, :], rt[...])
        square = pre * pre
        t = jnp.tanh(k0 * pre * (1.0 + k1 * square))
        half = 0.5 * (1.0 + t)
        slope[at, :] = half + (0.5 * k0) * pre * (1.0 - t * t) * (1.0 + (3.0 * k1) * square)
        hi, lo = split2(pre * half)
        made[at, :] = nt(hi, pxt_ref[:128]) + nt(lo, pxt_ref[:128])
        return carry

    lax.fori_loop(0, GA, forward, 0)

    wait_across(*tg_args)

    def backward(g, carry):
        at = pl.ds(pl.multiple_of(128 * g, 128), 128)
        hi, lo = split2(made[at, :] - transposed(rcv_tg[g]))
        d_pre = nn(jnp.concatenate([hi, lo], axis=1), pxt_ref[...]) * slope[at, :]
        hi, lo = split2(d_pre)
        dp_hi[at, :] = hi
        dp_lo[at, :] = lo
        return carry

    lax.fori_loop(0, GA, backward, 0)
    loads[6].wait()
    for t in range(2):
        cols = slice(256 * t, 256 * t + 256)
        both = nn(fjd[0], dp_hi[:, cols]) + nn(fjd[1], dp_hi[:, cols]) + nn(fjd[0], dp_lo[:, cols])
        ft[2 * t], ft[2 * t + 1] = both[:, :128], both[:, 128:]
    for t in range(4):
        src = [ft[t, pl.ds(32 * j, 32), :] for j in range(4)]
        for m in range(4):
            made_of = None
            for j in range(4):
                turn = (32 * (j - m)) % 128
                piece = pltpu.roll(src[j], turn, 1) if turn else src[j]
                made_of = piece if made_of is None else jnp.where(group == j, piece, made_of)
            snd_g[pl.ds(4 * t + m, 32, stride=16), :] = made_of
    g_args = (snd_g, rcv_g, g_send, g_recv, 16)
    exchange_rows(*g_args)
    wait_rows(*g_args)

    arrived = rcv_g[...].reshape(DEV, 2, 8, 128)
    hi, lo = split2(jnp.concatenate([arrived[:, h].reshape(256, 128) for h in range(2)], axis=0))
    turned = nn(cx[0], hi) + nn(cx[1], hi) + nn(cx[0], lo)
    cosine, sine = turned[:128].T, turned[128:].T
    for ky in range(2):
        re, im = slice(64 * ky, 64 * ky + 32), slice(64 * ky + 32, 64 * ky + 64)
        grads[ga, ky, 0] = cosine[re] + sine[im]
        grads[ga, ky, 1] = cosine[im] - sine[re]
    grads_args = (lambda g: grads.at[ga], grads, gm_send, gm_recv)
    start_across(*grads_args)
    wait_across(*modes_args)
    wait_across(*grads_args)
    for ky in range(2):
        factor = jnp.where(2 * dev + ky == 0, 1.0, 2.0).astype(F32) / (XC * YC)
        for c in range(3):
            out_re, out_im = 0.0, 0.0
            for b in range(GA):
                x_re = modes[b, 8 * ky + 2 * c : 8 * ky + 2 * c + 1, :]
                x_im = modes[b, 8 * ky + 2 * c + 1 : 8 * ky + 2 * c + 2, :]
                g_re, g_im = grads[b, ky, 0], grads[b, ky, 1]
                out_re = out_re + (x_re * g_re + x_im * g_im)
                out_im = out_im + (x_re * g_im - x_im * g_re)
            t_out[ky, 0, c] = out_re * factor
            t_out[ky, 1, c] = out_im * factor
    state_copy.wait()


def expand_kernel(lift_h, t_h, state_h, out_h, new_state_h, lift, t, state, lift_wide, out, sem):
    loads = [
        pltpu.make_async_copy(a, b, sem.at[n]) for n, (a, b) in enumerate(((lift_h, lift), (t_h, t), (state_h, state)))
    ]
    for c in loads:
        c.start()
    forward = pltpu.make_async_copy(state, new_state_h, sem.at[4])
    loads[0].wait()
    for c in range(3):
        lift_wide[c] = widened(lift[...], c)
    loads[1].wait()

    def stretch(n):
        ky, rest = n // 8, n % 8
        part, rows = rest // 4, pl.ds(8 * (rest % 4), 8)
        return pltpu.make_async_copy(out.at[ky, part, rows], out_h.at[ky, part, rows], sem.at[3])

    def body(n, carry):
        ky, rest = n // 8, n % 8
        part, first = rest // 4, 8 * (rest % 4)
        terms = [t[ky, part, c] for c in range(3)]
        for i in range(8):
            total = 0.0
            for c in range(3):
                total = total + jnp.broadcast_to(lift_wide[c, pl.ds(first + i, 1), :], (WIDTH, 128)) * terms[c]
            out[ky, part, first + i] = total
        stretch(n).start()
        return carry

    lax.fori_loop(0, 4, body, 0)
    loads[2].wait()
    forward.start()
    lax.fori_loop(4, 16, body, 0)

    pltpu.make_async_copy(out, out_h, sem.at[3]).wait()
    forward.wait()


def per_device(consts, density, velocity, pressure, lift, spectral, pointwise, project):
    hbm = pl.BlockSpec(memory_space=pl.ANY)
    V = pltpu.VMEM
    dma = pltpu.SemaphoreType.DMA
    field = V((5, 384, 128), F32)
    rows = V((512, 128), F32)
    coarse = V((GA, 48, 128), F32)
    scratch = [
        V((4, 32, 256), F32), V((3, 4, 32, 256), F32), V((4, 32, 256), F32), V((3, WIDTH), BF16), V((WIDTH, WIDTH), BF16),
        V((3, WIDTH), BF16), V((5, 4, 32, 256), F32), V((3, WIDTH, 128), F32),
        V((2, 2, WIDTH, WIDTH, 128), BF16), V((2, 128, 512), BF16), V((2, 128, 512), BF16), V((512, 384), BF16),
        V((2, 256, 512), BF16), V((2, 512, 256), BF16), V((256, 128), BF16),
        field, field, field, field, field, field, V((3, 5, 8, 384), F32),
        V((2, 5, 8, 128), F32), V((2, 2, 5, 8, 128), F32), V((2, 5, 8, 128), F32), V((4, 5, 8, 128), F32),
        V((384, 128), F32), coarse, coarse, coarse, coarse, V((256, 128), F32), V((256, 128), F32), rows, rows, rows, rows,
        V((2, 2, 3, WIDTH, 128), F32), V((GA, 16, 128), F32), V((GA, 2, 2, WIDTH, 128), F32),
        V((384, 512), BF16), V((512, 512), F32), V((512, 128), F32),
        V((512, 512), BF16), V((512, 512), BF16), V((4, 128, 128), F32), V((48, 512), F32), V((256, 512), BF16),
        dma((14,)), dma((4,)), dma((4,)), dma((1,)), dma((1,)), dma((1,)), dma((1,)),
        dma((1,)), dma((1,)), dma((1,)), dma((1,)), dma((1,)), dma((1,)),
        pltpu.SemaphoreType.REGULAR, dma((1,)), dma((1,)), dma((1,)), dma((1,)),
    ]
    new_state, t = pl.pallas_call(
        kernel,
        out_shape=(
            jax.ShapeDtypeStruct((5, 4, 32, 256), F32),
            jax.ShapeDtypeStruct((2, 2, 3, WIDTH, 128), F32),
        ),
        in_specs=[hbm] * 13,
        out_specs=(hbm, pl.BlockSpec(memory_space=pltpu.VMEM)),
        scratch_shapes=scratch,
        compiler_params=pltpu.CompilerParams(
            collective_id=0, has_side_effects=True, vmem_limit_bytes=VMEM_BYTES
        ),
    )(density, velocity, pressure, lift, pointwise, project.T, spectral, *consts)
    grad, new_state = pl.pallas_call(
        expand_kernel,
        out_shape=(
            jax.ShapeDtypeStruct((2, 2, WIDTH, WIDTH, 128), F32),
            jax.ShapeDtypeStruct((5, 4, 32, 256), F32),
        ),
        in_specs=[hbm] * 3,
        out_specs=(hbm, hbm),
        scratch_shapes=[
            V((3, WIDTH), BF16), V((2, 2, 3, WIDTH, 128), F32), V((5, 4, 32, 256), F32), V((3, WIDTH, 128), F32),
            V((2, 2, WIDTH, WIDTH, 128), F32), dma((5,)),
        ],
        compiler_params=pltpu.CompilerParams(vmem_limit_bytes=VMEM_BYTES),
    )(lift, t, new_state)
    return new_state, grad


def solution(mesh):
    in_specs = (
        P(None, "dev", "ga"),
        P(None, None, "dev", "ga"),
        P(None, "dev", "ga"),
        P(),
        P("dev", None, None, None, None),
        P(),
        P(),
    )
    out_specs = (P(None, None, "dev", "ga"), P("dev", None, None, None, None))

    def whole(*args):
        consts = tables()
        return jax.shard_map(
            lambda *a: per_device(a[:6], *a[6:]),
            mesh=mesh, in_specs=(P(),) * 6 + in_specs, out_specs=out_specs, check_vma=False,
        )(*[jnp.asarray(c) for c in consts], *args)

    return whole
```

```python
import functools
import math

import jax
import jax.numpy as jnp
import numpy as np
from jax import lax
from jax.experimental import pallas as pl
from jax.experimental.pallas import tpu as pltpu
from jax.sharding import PartitionSpec as P

MESH = pl.DeviceIdType.MESH
F32 = jnp.float32
BF16 = jnp.bfloat16
WIDTH = 32
MODES = 64
XC = 512
YC = 512
GA = 4
DEV = 32
DT = 0.12
BLOCK = 8
OFFSETS = sorted(
    ((a, b, c) for a in range(4) for b in range(4) for c in range(2) if a + b + c),
    key=lambda o: (-min(o[0], 4 - o[0]) - min(o[1], 4 - o[1]), o),
)
VMEM_BYTES = 62 * 1024 * 1024


def tables():
    def split(a):
        a = np.asarray(a, np.float32)
        hi = a.astype(jnp.bfloat16)
        lo = (a - hi.astype(np.float32)).astype(jnp.bfloat16)
        return np.ascontiguousarray(np.stack([hi, lo]))

    ky = np.arange(MODES)
    y = np.arange(YC)
    ang = 2 * np.pi * ((ky[:, None] * y[None, :]) % YC) / YC
    fwd = np.stack([np.cos(ang), -np.sin(ang)], axis=1)
    weight = np.where(ky == 0, 1.0, 2.0) / (XC * YC)
    inv = fwd * weight[:, None, None]
    fwd_dj = fwd.reshape(DEV, 4, YC)
    fwd_jd = fwd_dj.transpose(1, 0, 2).reshape(128, YC)
    inv_jd = inv.reshape(DEV, 4, YC).transpose(1, 0, 2).reshape(128, YC).T
    q = np.arange(2 * MODES)
    kx = np.where(q < MODES, q, XC - 2 * MODES + q)
    ax = 2 * np.pi * ((kx[:, None] * np.arange(XC)[None, :]) % XC) / XC
    cx = np.concatenate([np.cos(ax), np.sin(ax)], axis=0)
    cx_halves = cx.reshape(256, DEV, 2, 8).transpose(0, 2, 1, 3).reshape(256, XC)
    inv_hi, inv_lo = split(inv_jd)

    pool = np.zeros((256, 128), np.float32)
    pool[np.arange(256), np.arange(256) // 2] = 0.25
    return (
        split(fwd_dj.reshape(128, YC)),
        split(fwd_jd),
        np.concatenate([inv_hi, inv_hi, inv_lo], axis=1),
        split(cx_halves),
        split(cx.T),
        pool.astype(jnp.bfloat16),
    )


def split2(a):
    hi = a.astype(BF16)
    return hi, (a - hi.astype(F32)).astype(BF16)


def nn(a, b):
    return lax.dot_general(a, b, (((1,), (0,)), ((), ())), preferred_element_type=F32)


def nt(a, b):
    return lax.dot_general(a, b, (((1,), (1,)), ((), ())), preferred_element_type=F32)


def tn(a, b):
    return lax.dot_general(a, b, (((0,), (0,)), ((), ())), preferred_element_type=F32)


def primitives(u):
    inv = 1.0 / u[0]
    v = [u[1] * inv, u[2] * inv, u[3] * inv]
    kinetic = u[1] * v[0] + u[2] * v[1] + u[3] * v[2]
    p = 0.4 * (u[4] - 0.5 * kinetic)
    sound = jnp.sqrt(1.4 * p * inv)
    return v, p, sound


def directional(u, v, p, sound, d):
    n = v[d]
    flux = [u[1 + d]]
    for i in range(3):
        f = u[1 + i] * n
        flux.append(f + p if i == d else f)
    flux.append((u[4] + p) * n)
    return flux, jnp.abs(n) + sound


def faces(ul, ur, fl, fr, sl, sr):
    top = jnp.maximum(sl, sr)
    return [(a + b) - top * (d - c) for a, b, c, d in zip(fl, fr, ul, ur)]


def widened(lift, c):
    pick = (lax.broadcasted_iota(jnp.int32, (3, 128), 0) == c).astype(F32).astype(BF16)
    return tn(lift, pick)


def rim_rates(u):
    v, p, sound = primitives(u)
    total, along_y = None, None
    for d, (axis, step, size) in enumerate(((0, 2, 8), (1, 8, 384), (1, 1, 384))):
        flux, speed = directional(u, v, p, sound, d)

        def up(a):
            return pltpu.roll(a, size - step, axis)

        g = faces(u, [up(a) for a in u], flux, [up(a) for a in flux], speed, up(speed))
        div = [a - pltpu.roll(a, step, axis) for a in g]
        total = div if total is None else [a + b for a, b in zip(total, div)]
        along_y = g
    return total, along_y


def block_rates(src, edge, r0):
    lane = lax.broadcasted_iota(jnp.int32, (BLOCK, 8, 128), 2)
    odd = lax.broadcasted_iota(jnp.int32, (BLOCK, 8, 128), 1) % 2 == 1
    last = lane == 127
    base = pl.multiple_of(8 * (r0 - 1), 8)
    wide = [src[f, pl.ds(base, 8 * BLOCK + 16), :].reshape(BLOCK + 2, 8, 128) for f in range(5)]
    v, p, sound = primitives(wide)
    flux, speed = directional(wide, v, p, sound, 1)
    g = faces(
        [a[:-1] for a in wide], [a[1:] for a in wide], [a[:-1] for a in flux], [a[1:] for a in flux], speed[:-1], speed[1:]
    )
    total = [a[1:] - a[:-1] for a in g]
    u = [a[1:-1] for a in wide]
    v = [a[1:-1] for a in v]
    p, sound = p[1:-1], sound[1:-1]

    flux, speed = directional(u, v, p, sound, 0)

    def up_z(a):
        return pltpu.roll(a, 6, 1)

    g = faces(u, [up_z(a) for a in u], flux, [up_z(a) for a in flux], speed, up_z(speed))
    total = [t + (a - pltpu.roll(a, 2, 1)) for t, a in zip(total, g)]

    flux, speed = directional(u, v, p, sound, 2)

    def up_y(a):
        near = pltpu.roll(a, 127, 2)
        return jnp.where(last, pltpu.roll(near, 7, 1), near)

    g = faces(u, [up_y(a) for a in u], flux, [up_y(a) for a in flux], speed, up_y(speed))
    at = pl.multiple_of(8 * r0, 8)
    for f in range(5):
        outer = edge[f, pl.ds(at, 8 * BLOCK), :].reshape(BLOCK, 8, 128)
        upper = jnp.where(last & odd, outer, g[f])
        wrapped = jnp.where(odd, pltpu.roll(g[f], 1, 1), outer)
        lower = pltpu.roll(jnp.where(last, wrapped, g[f]), 1, 2)
        total[f] = total[f] + (upper - lower)
    return total


def kernel(
    density_h, velocity_h, pressure_h, lift_h, pointwise_h, project_h, spectral_h,
    fdj_h, fjd_h, inv_h, cx_h, cxt_h, pool_h,
    new_state_h, t_out,
    density, velocity, pressure, lift, pointwise, project, new_state, lift_wide,
    spectral, fdj, fjd, inv, cx, cxt, pool,
    u0, ua, ub, uc, acc, edge, rim, own_edge, side_edge, row_edge, corner_edge,
    pooled, snd_in, rcv_in, snd_tg, rcv_tg, snd_x, rcv_x, snd_b, rcv_b, snd_g, rcv_g,
    contracted, modes, grads, rt, slope, made, dp_hi, dp_lo, ft, lpx_ref, pxt_ref,
    load_sem, halo_send, halo_recv, in_send, in_recv, tg_send, tg_recv, x_send, x_recv, b_send, b_recv,
    g_send, g_recv, relay, xm_send, xm_recv, gm_send, gm_recv,
):
    ga = lax.axis_index("ga")
    dev = lax.axis_index("dev")
    east, west = lax.rem(ga + 1, GA), lax.rem(ga + GA - 1, GA)
    south, north = lax.rem(dev + 1, DEV), lax.rem(dev + DEV - 1, DEV)

    loads = [
        pltpu.make_async_copy(a, b, load_sem.at[n])
        for n, (a, b) in enumerate(
            (
                (pool_h, pool), (spectral_h, spectral), (fdj_h, fdj), (cx_h, cx), (cxt_h, cxt), (inv_h, inv), (fjd_h, fjd),
                (density_h, density), (velocity_h, velocity), (pressure_h, pressure),
                (lift_h, lift), (pointwise_h, pointwise), (project_h, project),
            )
        )
    ]
    for n in (7, 8, 9, 0, 10, 11, 12, 1, 2, 3, 4, 5, 6):
        loads[n].start()

    barrier = pltpu.get_barrier_semaphore()

    core, chip_x, chip_y = lax.rem(dev, 2), lax.rem(lax.div(dev, 2), 4), lax.div(dev, 8)

    def at(dy, dx, dc):
        return lax.rem(chip_y + dy, 4) * 8 + lax.rem(chip_x + dx, 4) * 2 + lax.rem(core + dc, 2)

    beside = jnp.where(core == 1, south, north)
    line_x = [(ga, at(0, k, 0)) for k in range(1, 4)]
    first = [(lax.rem(ga + k, GA), dev) for k in range(1, GA)]
    first += [(ga, at(a, 0, c)) for a in range(4) for c in range(2) if a + c] + line_x + [(ga, beside)]
    for who in first:
        pl.semaphore_signal(barrier, inc=1, device_id=who, device_id_type=MESH)

    def exchange_rows(snd, rcv, ssem, rsem, unit):
        for dy, dx, dc in OFFSETS:
            peer = at(dy, dx, dc)
            pltpu.make_async_remote_copy(
                src_ref=snd.at[pl.ds(pl.multiple_of(unit * peer, unit), unit)],
                dst_ref=rcv.at[pl.ds(pl.multiple_of(unit * dev, unit), unit)],
                send_sem=ssem.at[0], recv_sem=rsem.at[0],
                device_id=(ga, peer), device_id_type=MESH,
            ).start()
        mine = pl.ds(pl.multiple_of(unit * dev, unit), unit)
        rcv[mine, :] = snd[mine, :]

    def wait_rows(snd, rcv, ssem, rsem, unit):
        whole = pl.ds(0, unit * (DEV - 1))
        pltpu.make_async_remote_copy(
            src_ref=snd.at[whole], dst_ref=rcv.at[whole], send_sem=ssem.at[0], recv_sem=rsem.at[0],
            device_id=(ga, south), device_id_type=MESH,
        ).wait()

    def start_across(src, dst, ssem, rsem):
        for k in (2, 1, 3):
            peer = lax.rem(ga + k, GA)
            pltpu.make_async_remote_copy(
                src_ref=src(peer), dst_ref=dst.at[ga], send_sem=ssem.at[0], recv_sem=rsem.at[0],
                device_id=(peer, dev), device_id_type=MESH,
            ).start()

    def wait_across(src, dst, ssem, rsem):
        three = dst.at[pl.ds(0, GA - 1)]
        pltpu.make_async_remote_copy(
            src_ref=three, dst_ref=three, send_sem=ssem.at[0], recv_sem=rsem.at[0],
            device_id=(east, dev), device_id_type=MESH,
        ).wait()

    def coarsen(rows, snd):
        hi, lo = split2(rows)
        pooled[...] = nn(hi, pool[...]) + nn(lo, pool[...])
        both = pooled[pl.ds(0, 192, stride=2), :] + pooled[pl.ds(1, 192, stride=2), :]
        snd[...] = both.reshape(GA, 48, 128)

    for n in (7, 8, 9):
        loads[n].wait()
    for p in range(4):
        for h in range(2):
            cols = slice(128 * h, 128 * h + 128)
            rho = density[p, :, cols]
            v = [velocity[c, p, :, cols] for c in range(3)]
            where = pl.ds(32 + 2 * p + h, 32, stride=8)
            u0[0, where, :] = rho
            for c in range(3):
                u0[1 + c, where, :] = rho * v[c]
            u0[4, where, :] = pressure[p, :, cols] / 0.4 + 0.5 * rho * (v[0] * v[0] + v[1] * v[1] + v[2] * v[2])

    lane1 = lax.broadcasted_iota(jnp.int32, (8, 128), 1)
    for w in range(2):
        for f in range(5):
            packed = None
            for k in range(16):
                row = pltpu.roll(u0[f, pl.ds(8 * (16 * w + k + 4), 8), :], (4 + 8 * k) % 128, 1)
                packed = row if packed is None else jnp.where(lane1 >= 8 * k, row, packed)
            own_edge[w, f] = packed

    loads[0].wait()
    coarsen(jnp.concatenate([velocity[c, p] for p in range(4) for c in range(3)], axis=0), snd_in)

    pl.semaphore_wait(barrier, len(first))
    second = line_x + [(east, dev), (west, dev)]
    for who in second:
        pl.semaphore_signal(relay, inc=1, device_id=who, device_id_type=MESH)

    def halo(n, src, dst, target):
        return pltpu.make_async_remote_copy(
            src_ref=src, dst_ref=dst, send_sem=halo_send.at[n], recv_sem=halo_recv.at[n],
            device_id=target, device_id_type=MESH,
        )

    halos = [
        halo(0, u0.at[:, pl.ds(8 * 32, 32)], u0.at[:, pl.ds(0, 32)], (ga, south)),
        halo(0, u0.at[:, pl.ds(8 * 4, 32)], u0.at[:, pl.ds(8 * 36, 32)], (ga, north)),
        halo(2, own_edge, side_edge.at[0], (east, dev)),
        halo(2, own_edge, side_edge.at[1], (west, dev)),
        halo(1, own_edge.at[1], row_edge.at[0], (ga, south)),
        halo(1, own_edge.at[0], row_edge.at[1], (ga, north)),
    ]
    corners = [
        halo(3, own_edge.at[1], corner_edge.at[0], (east, south)),
        halo(3, own_edge.at[0], corner_edge.at[1], (east, north)),
        halo(3, own_edge.at[1], corner_edge.at[2], (west, south)),
        halo(3, own_edge.at[0], corner_edge.at[3], (west, north)),
    ]
    halo_waits = [
        halo(n, a, a, (ga, south)) for n, a in enumerate((u0.at[:, pl.ds(0, 64)], row_edge, side_edge, corner_edge))
    ]
    in_args = (lambda g: snd_in.at[g], rcv_in, in_send, in_recv)
    start_across(*in_args)
    for c in halos:
        c.start()
    rcv_in[ga] = snd_in[ga]

    for n in (10, 11, 12, 1):
        loads[n].wait()
    for c in range(3):
        lift_wide[c] = widened(lift[...], c)
    for ky in range(2):
        for part in range(2):

            def add(w8, total, ky=ky, part=part):
                total = list(total)
                for n in range(4):
                    w = 4 * w8 + n
                    s = spectral[ky, part, w].astype(F32)
                    for c in range(3):
                        total[c] = total[c] + jnp.broadcast_to(lift_wide[c, pl.ds(w, 1), :], (WIDTH, 128)) * s
                return tuple(total)

            zero = jnp.zeros((WIDTH, 128), F32)
            done = lax.fori_loop(0, WIDTH // 4, add, (zero, zero, zero))
            for c in range(3):
                contracted[ky, part, c] = done[c]

    tile_o = (
        lax.broadcasted_iota(jnp.int32, (WIDTH, 512), 1) % WIDTH == lax.broadcasted_iota(jnp.int32, (WIDTH, 512), 0)
    ).astype(F32).astype(BF16)
    same_row = (
        lax.broadcasted_iota(jnp.int32, (48, 512), 1) // WIDTH == lax.broadcasted_iota(jnp.int32, (48, 512), 0) % 16
    )

    def spread(a):
        return jnp.where(
            same_row, jnp.concatenate([jnp.broadcast_to(a[c : c + 1], (16, 512)) for c in range(3)], axis=0), 0.0
        )

    lp_hi, lp_lo = split2(nn(lift[...], pointwise[...]))
    lpx_ref[...] = spread(nn(lp_hi, tile_o) + nn(lp_lo, tile_o))
    spread_out = jnp.concatenate([spread(nn(project[...], tile_o)), jnp.zeros((80, 512), F32)], axis=0)
    pxt_ref[...] = jnp.concatenate([spread_out, spread_out], axis=0).astype(BF16)

    pl.semaphore_wait(relay, len(second))
    for c in corners:
        c.start()

    wait_across(*in_args)
    loads[2].wait()
    hi, lo = split2(jnp.concatenate([rcv_in[g] for g in range(GA)], axis=1))
    freq = nt(hi, fdj[0]) + nt(hi, fdj[1]) + nt(lo, fdj[0])
    for d in range(DEV):
        packed = None
        for n in range(6):
            h, c = n // 3, n % 3
            piece = pltpu.roll(freq[16 * c + 8 * h : 16 * c + 8 * h + 8], (16 * h + 4 * c - 4 * d) % 128, 1)
            packed = piece if packed is None else jnp.where(lane1 >= 16 * h + 4 * c, piece, packed)
        snd_x[pl.ds(8 * d, 8), :] = packed
    x_args = (snd_x, rcv_x, x_send, x_recv, 8)
    exchange_rows(*x_args)

    sub1 = lax.broadcasted_iota(jnp.int32, (8, 128), 0)
    even, outside = sub1 % 2 == 0, lane1 % 8 < 4
    low = lane1 < 64

    def fill_rim(n, f, own, left, right):
        rim[0, f, :, 128 * n : 128 * n + 128] = jnp.where(
            even, jnp.where(outside, pltpu.roll(left, 7, 0), own), jnp.where(outside, own, pltpu.roll(right, 1, 0))
        )

    def stage(src, dst, ahead, first_row, last_row, rim_src, rim_dst, stride=BLOCK):
        total, along_y = rim_rates([rim[rim_src, f] for f in range(5)])
        for f in range(5):
            if rim_dst is not None:
                rim[rim_dst, f] = rim[0, f] - (0.5 * ahead) * total[f]
            for n in range(3):
                for k in range(16):
                    edge[f, pl.ds(8 * ((16 * n + k + 4) % 48), 8), :] = pltpu.roll(
                        along_y[f][:, 128 * n : 128 * n + 128], 124 - 8 * k, 1
                    )

        def block(n, carry):
            r0 = jnp.minimum(first_row + stride * n, last_row + 1 - BLOCK)
            total = block_rates(src, edge, r0)
            at = pl.ds(pl.multiple_of(8 * r0, 8), 8 * BLOCK)
            for f in range(5):
                t = total[f].reshape(8 * BLOCK, 128)
                if dst is not None:
                    dst[f, at, :] = u0[f, at, :] - (0.5 * ahead) * t
                else:
                    mean = (ua[f, at, :] + 2.0 * ub[f, at, :] + uc[f, at, :] - u0[f, at, :]) * (1.0 / 3.0)
                    acc[f, at, :] = mean - (DT / 12.0) * t
            return carry

        lax.fori_loop(0, -(-(last_row + 1 - first_row) // stride), block, 0)

    halo_waits[2].wait()
    for f in range(5):
        for n in range(2):
            fill_rim(n, f, own_edge[n, f], side_edge[0, n, f], side_edge[1, n, f])
        fill_rim(2, f, own_edge[0, f], side_edge[0, 0, f], side_edge[1, 0, f])
    stage(u0, ua, 0.5 * DT, 5, 34, 0, None)
    for n in (0, 1, 3):
        halo_waits[n].wait()
    for f in range(5):
        fill_rim(
            2, f, jnp.where(low, row_edge[1, f], row_edge[0, f]),
            jnp.where(low, corner_edge[1, f], corner_edge[0, f]), jnp.where(low, corner_edge[3, f], corner_edge[2, f]),
        )
    stage(u0, ua, 0.5 * DT, 1, 38, 0, 1, 30)
    stage(ua, ub, 0.5 * DT, 2, 37, 1, 2)

    wait_rows(*x_args)
    loads[3].wait()
    hi, lo = split2(rcv_x[...])
    turned = 0.0
    for h in range(2):
        cols = slice(256 * h, 256 * h + 256)
        half = nn(cx[0, :, cols], hi) + nn(cx[1, :, cols], hi) + nn(cx[0, :, cols], lo)
        turned = turned + (pltpu.roll(half, 112, 1) if h else half)
    cosine, sine = turned[:128].T, turned[128:].T
    for ky in range(2):
        for c in range(3):
            r = 4 * c + 2 * ky
            modes[ga, 8 * ky + 2 * c : 8 * ky + 2 * c + 1, :] = cosine[r : r + 1] + sine[r + 1 : r + 2]
            modes[ga, 8 * ky + 2 * c + 1 : 8 * ky + 2 * c + 2, :] = cosine[r + 1 : r + 2] - sine[r : r + 1]
        modes[ga, 8 * ky + 6 : 8 * ky + 8, :] = jnp.zeros((2, 128), F32)
    modes_args = (lambda g: modes.at[ga], modes, xm_send, xm_recv)
    start_across(*modes_args)
    mine = modes[ga]
    rows = []
    for ky in range(2):
        out_re, out_im = 0.0, 0.0
        for c in range(3):
            a = mine[8 * ky + 2 * c : 8 * ky + 2 * c + 1]
            b = mine[8 * ky + 2 * c + 1 : 8 * ky + 2 * c + 2]
            re, im = contracted[ky, 0, c], contracted[ky, 1, c]
            out_re = out_re + (a * re - b * im)
            out_im = out_im + (a * im + b * re)
        rows.append(jnp.concatenate([out_re, -out_im], axis=1))
        rows.append(jnp.concatenate([out_im, out_re], axis=1))
    hi, lo = split2(jnp.concatenate(rows, axis=0))
    loads[4].wait()
    snd_b[...] = nt(cxt[0], hi) + nt(cxt[1], hi) + nt(cxt[0], lo)
    b_args = (snd_b, rcv_b, b_send, b_recv, 16)
    exchange_rows(*b_args)

    stage(ub, uc, DT, 3, 36, 2, 1)
    stage(uc, None, DT, 4, 35, 1, None)

    after = []
    for p in range(4):
        parts = []
        for h in range(2):
            where = pl.ds(32 + 2 * p + h, 32, stride=8)
            cols = slice(128 * h, 128 * h + 128)
            u = [acc[f, where, :] for f in range(5)]
            for f in range(5):
                new_state[f, p, :, cols] = u[f]
            inv_rho = 1.0 / u[0]
            parts.append([u[1 + c] * inv_rho for c in range(3)])
        for c in range(3):
            after.append(jnp.concatenate([parts[0][c], parts[1][c]], axis=1))
    coarsen(jnp.concatenate(after, axis=0), snd_tg)
    state_copy = pltpu.make_async_copy(new_state, new_state_h, load_sem.at[13])
    state_copy.start()
    tg_args = (lambda g: snd_tg.at[g], rcv_tg, tg_send, tg_recv)
    start_across(*tg_args)
    rcv_tg[ga] = snd_tg[ga]

    lpx_hi, lpx_lo = split2(lpx_ref[...])

    def transposed(a):
        return jnp.concatenate([a, jnp.zeros((80, 128), F32)], axis=0).T

    for g in range(GA):
        ins_hi, ins_lo = split2(transposed(rcv_in[g])[:, :48])
        slope[pl.ds(128 * g, 128), :] = nn(ins_hi, lpx_hi) + nn(ins_hi, lpx_lo) + nn(ins_lo, lpx_hi)

    wait_rows(*b_args)
    loads[5].wait()
    group = lax.broadcasted_iota(jnp.int32, (32, 128), 1) // 32
    for t in range(4):
        src = [rcv_b[pl.ds(4 * t + m, 32, stride=16), :] for m in range(4)]
        for j in range(4):
            made_of = None
            for m in range(4):
                turn = (32 * (m - j)) % 128
                piece = pltpu.roll(src[m], turn, 1) if turn else src[m]
                made_of = piece if made_of is None else jnp.where(group == m, piece, made_of)
            hi, lo = split2(made_of)
            for n, piece in enumerate((hi, lo, hi)):
                rt[pl.ds(128 * n + 32 * j, 32), 128 * t : 128 * t + 128] = piece

    k0, k1 = math.sqrt(2.0 / math.pi), 0.044715

    def forward(g, carry):
        at = pl.ds(pl.multiple_of(128 * g, 128), 128)
        pre = slope[at, :] + nn(inv[at, :], rt[...])
        square = pre * pre
        t = jnp.tanh(k0 * pre * (1.0 + k1 * square))
        half = 0.5 * (1.0 + t)
        slope[at, :] = half + (0.5 * k0) * pre * (1.0 - t * t) * (1.0 + (3.0 * k1) * square)
        hi, lo = split2(pre * half)
        made[at, :] = nt(hi, pxt_ref[:128]) + nt(lo, pxt_ref[:128])
        return carry

    lax.fori_loop(0, GA, forward, 0)

    wait_across(*tg_args)

    def backward(g, carry):
        at = pl.ds(pl.multiple_of(128 * g, 128), 128)
        hi, lo = split2(made[at, :] - transposed(rcv_tg[g]))
        d_pre = nn(jnp.concatenate([hi, lo], axis=1), pxt_ref[...]) * slope[at, :]
        hi, lo = split2(d_pre)
        dp_hi[at, :] = hi
        dp_lo[at, :] = lo
        return carry

    lax.fori_loop(0, GA, backward, 0)
    loads[6].wait()
    for t in range(2):
        cols = slice(256 * t, 256 * t + 256)
        both = nn(fjd[0], dp_hi[:, cols]) + nn(fjd[1], dp_hi[:, cols]) + nn(fjd[0], dp_lo[:, cols])
        ft[2 * t], ft[2 * t + 1] = both[:, :128], both[:, 128:]
    for t in range(4):
        src = [ft[t, pl.ds(32 * j, 32), :] for j in range(4)]
        for m in range(4):
            made_of = None
            for j in range(4):
                turn = (32 * (j - m)) % 128
                piece = pltpu.roll(src[j], turn, 1) if turn else src[j]
                made_of = piece if made_of is None else jnp.where(group == j, piece, made_of)
            snd_g[pl.ds(4 * t + m, 32, stride=16), :] = made_of
    g_args = (snd_g, rcv_g, g_send, g_recv, 16)
    exchange_rows(*g_args)
    wait_rows(*g_args)

    arrived = rcv_g[...].reshape(DEV, 2, 8, 128)
    hi, lo = split2(jnp.concatenate([arrived[:, h].reshape(256, 128) for h in range(2)], axis=0))
    turned = nn(cx[0], hi) + nn(cx[1], hi) + nn(cx[0], lo)
    cosine, sine = turned[:128].T, turned[128:].T
    for ky in range(2):
        re, im = slice(64 * ky, 64 * ky + 32), slice(64 * ky + 32, 64 * ky + 64)
        grads[ga, ky, 0] = cosine[re] + sine[im]
        grads[ga, ky, 1] = cosine[im] - sine[re]
    grads_args = (lambda g: grads.at[ga], grads, gm_send, gm_recv)
    start_across(*grads_args)
    wait_across(*modes_args)
    wait_across(*grads_args)
    for ky in range(2):
        factor = jnp.where(2 * dev + ky == 0, 1.0, 2.0).astype(F32) / (XC * YC)
        for c in range(3):
            out_re, out_im = 0.0, 0.0
            for b in range(GA):
                x_re = modes[b, 8 * ky + 2 * c : 8 * ky + 2 * c + 1, :]
                x_im = modes[b, 8 * ky + 2 * c + 1 : 8 * ky + 2 * c + 2, :]
                g_re, g_im = grads[b, ky, 0], grads[b, ky, 1]
                out_re = out_re + (x_re * g_re + x_im * g_im)
                out_im = out_im + (x_re * g_im - x_im * g_re)
            t_out[ky, 0, c] = out_re * factor
            t_out[ky, 1, c] = out_im * factor
    state_copy.wait()


def expand_kernel(lift_h, t_h, state_h, out_h, new_state_h, lift, t, state, lift_wide, out, sem):
    loads = [
        pltpu.make_async_copy(a, b, sem.at[n]) for n, (a, b) in enumerate(((lift_h, lift), (t_h, t), (state_h, state)))
    ]
    for c in loads:
        c.start()
    forward = pltpu.make_async_copy(state, new_state_h, sem.at[4])
    loads[0].wait()
    for c in range(3):
        lift_wide[c] = widened(lift[...], c)
    loads[1].wait()

    def stretch(n):
        ky, rest = n // 8, n % 8
        part, rows = rest // 4, pl.ds(8 * (rest % 4), 8)
        return pltpu.make_async_copy(out.at[ky, part, rows], out_h.at[ky, part, rows], sem.at[3])

    def body(n, carry):
        ky, rest = n // 8, n % 8
        part, first = rest // 4, 8 * (rest % 4)
        terms = [t[ky, part, c] for c in range(3)]
        for i in range(8):
            total = 0.0
            for c in range(3):
                total = total + jnp.broadcast_to(lift_wide[c, pl.ds(first + i, 1), :], (WIDTH, 128)) * terms[c]
            out[ky, part, first + i] = total
        stretch(n).start()
        return carry

    lax.fori_loop(0, 4, body, 0)
    loads[2].wait()
    forward.start()
    lax.fori_loop(4, 16, body, 0)

    pltpu.make_async_copy(out, out_h, sem.at[3]).wait()
    forward.wait()


def per_device(consts, density, velocity, pressure, lift, spectral, pointwise, project):
    hbm = pl.BlockSpec(memory_space=pl.ANY)
    V = pltpu.VMEM
    dma = pltpu.SemaphoreType.DMA
    field = V((5, 384, 128), F32)
    rows = V((512, 128), F32)
    coarse = V((GA, 48, 128), F32)
    scratch = [
        V((4, 32, 256), F32), V((3, 4, 32, 256), F32), V((4, 32, 256), F32), V((3, WIDTH), BF16), V((WIDTH, WIDTH), BF16),
        V((3, WIDTH), BF16), V((5, 4, 32, 256), F32), V((3, WIDTH, 128), F32),
        V((2, 2, WIDTH, WIDTH, 128), BF16), V((2, 128, 512), BF16), V((2, 128, 512), BF16), V((512, 384), BF16),
        V((2, 256, 512), BF16), V((2, 512, 256), BF16), V((256, 128), BF16),
        field, field, field, field, field, field, V((3, 5, 8, 384), F32),
        V((2, 5, 8, 128), F32), V((2, 2, 5, 8, 128), F32), V((2, 5, 8, 128), F32), V((4, 5, 8, 128), F32),
        V((384, 128), F32), coarse, coarse, coarse, coarse, V((256, 128), F32), V((256, 128), F32), rows, rows, rows, rows,
        V((2, 2, 3, WIDTH, 128), F32), V((GA, 16, 128), F32), V((GA, 2, 2, WIDTH, 128), F32),
        V((384, 512), BF16), V((512, 512), F32), V((512, 128), F32),
        V((512, 512), BF16), V((512, 512), BF16), V((4, 128, 128), F32), V((48, 512), F32), V((256, 512), BF16),
        dma((14,)), dma((4,)), dma((4,)), dma((1,)), dma((1,)), dma((1,)), dma((1,)),
        dma((1,)), dma((1,)), dma((1,)), dma((1,)), dma((1,)), dma((1,)),
        pltpu.SemaphoreType.REGULAR, dma((1,)), dma((1,)), dma((1,)), dma((1,)),
    ]
    new_state, t = pl.pallas_call(
        kernel,
        out_shape=(
            jax.ShapeDtypeStruct((5, 4, 32, 256), F32),
            jax.ShapeDtypeStruct((2, 2, 3, WIDTH, 128), F32),
        ),
        in_specs=[hbm] * 13,
        out_specs=(hbm, pl.BlockSpec(memory_space=pltpu.VMEM)),
        scratch_shapes=scratch,
        compiler_params=pltpu.CompilerParams(
            collective_id=0, has_side_effects=True, vmem_limit_bytes=VMEM_BYTES
        ),
    )(density, velocity, pressure, lift, pointwise, project.T, spectral, *consts)
    grad, new_state = pl.pallas_call(
        expand_kernel,
        out_shape=(
            jax.ShapeDtypeStruct((2, 2, WIDTH, WIDTH, 128), F32),
            jax.ShapeDtypeStruct((5, 4, 32, 256), F32),
        ),
        in_specs=[hbm] * 3,
        out_specs=(hbm, hbm),
        scratch_shapes=[
            V((3, WIDTH), BF16), V((2, 2, 3, WIDTH, 128), F32), V((5, 4, 32, 256), F32), V((3, WIDTH, 128), F32),
            V((2, 2, WIDTH, WIDTH, 128), F32), dma((5,)),
        ],
        compiler_params=pltpu.CompilerParams(vmem_limit_bytes=VMEM_BYTES),
    )(lift, t, new_state)
    return new_state, grad


def solution(mesh):
    in_specs = (
        P(None, "dev", "ga"),
        P(None, None, "dev", "ga"),
        P(None, "dev", "ga"),
        P(),
        P("dev", None, None, None, None),
        P(),
        P(),
    )
    out_specs = (P(None, None, "dev", "ga"), P("dev", None, None, None, None))

    def whole(*args):
        consts = tables()
        return jax.shard_map(
            lambda *a: per_device(a[:6], *a[6:]),
            mesh=mesh, in_specs=(P(),) * 6 + in_specs, out_specs=out_specs, check_vma=False,
        )(*[jnp.asarray(c) for c in consts], *args)

    return whole
```

```python
import functools
import math

import jax
import jax.numpy as jnp
import numpy as np
from jax import lax
from jax.experimental import pallas as pl
from jax.experimental.pallas import tpu as pltpu
from jax.sharding import PartitionSpec as P

MESH = pl.DeviceIdType.MESH
F32 = jnp.float32
BF16 = jnp.bfloat16
WIDTH = 32
MODES = 64
XC = 512
YC = 512
GA = 4
DEV = 32
DT = 0.12
BLOCK = 8
OFFSETS = sorted(
    ((a, b, c) for a in range(4) for b in range(4) for c in range(2) if a + b + c),
    key=lambda o: (-min(o[0], 4 - o[0]) - min(o[1], 4 - o[1]), o),
)
VMEM_BYTES = 62 * 1024 * 1024


def tables():
    def split(a):
        a = np.asarray(a, np.float32)
        hi = a.astype(jnp.bfloat16)
        lo = (a - hi.astype(np.float32)).astype(jnp.bfloat16)
        return np.ascontiguousarray(np.stack([hi, lo]))

    ky = np.arange(MODES)
    y = np.arange(YC)
    ang = 2 * np.pi * ((ky[:, None] * y[None, :]) % YC) / YC
    fwd = np.stack([np.cos(ang), -np.sin(ang)], axis=1)
    weight = np.where(ky == 0, 1.0, 2.0) / (XC * YC)
    inv = fwd * weight[:, None, None]
    fwd_dj = fwd.reshape(DEV, 4, YC)
    fwd_jd = fwd_dj.transpose(1, 0, 2).reshape(128, YC)
    inv_jd = inv.reshape(DEV, 4, YC).transpose(1, 0, 2).reshape(128, YC).T
    q = np.arange(2 * MODES)
    kx = np.where(q < MODES, q, XC - 2 * MODES + q)
    ax = 2 * np.pi * ((kx[:, None] * np.arange(XC)[None, :]) % XC) / XC
    cx = np.concatenate([np.cos(ax), np.sin(ax)], axis=0)
    cx_halves = cx.reshape(256, DEV, 2, 8).transpose(0, 2, 1, 3).reshape(256, XC)
    inv_hi, inv_lo = split(inv_jd)

    pool = np.zeros((256, 128), np.float32)
    pool[np.arange(256), np.arange(256) // 2] = 0.25
    return (
        split(fwd_dj.reshape(128, YC)),
        split(fwd_jd),
        np.concatenate([inv_hi, inv_hi, inv_lo], axis=1),
        split(cx_halves),
        split(cx.T),
        pool.astype(jnp.bfloat16),
    )


def split2(a):
    hi = a.astype(BF16)
    return hi, (a - hi.astype(F32)).astype(BF16)


def nn(a, b):
    return lax.dot_general(a, b, (((1,), (0,)), ((), ())), preferred_element_type=F32)


def nt(a, b):
    return lax.dot_general(a, b, (((1,), (1,)), ((), ())), preferred_element_type=F32)


def tn(a, b):
    return lax.dot_general(a, b, (((0,), (0,)), ((), ())), preferred_element_type=F32)


def primitives(u):
    inv = 1.0 / u[0]
    v = [u[1] * inv, u[2] * inv, u[3] * inv]
    kinetic = u[1] * v[0] + u[2] * v[1] + u[3] * v[2]
    p = 0.4 * (u[4] - 0.5 * kinetic)
    sound = jnp.sqrt(1.4 * p * inv)
    return v, p, sound


def directional(u, v, p, sound, d):
    n = v[d]
    flux = [u[1 + d]]
    for i in range(3):
        f = u[1 + i] * n
        flux.append(f + p if i == d else f)
    flux.append((u[4] + p) * n)
    return flux, jnp.abs(n) + sound


def faces(ul, ur, fl, fr, sl, sr):
    top = jnp.maximum(sl, sr)
    return [(a + b) - top * (d - c) for a, b, c, d in zip(fl, fr, ul, ur)]


def widened(lift, c):
    pick = (lax.broadcasted_iota(jnp.int32, (3, 128), 0) == c).astype(F32).astype(BF16)
    return tn(lift, pick)


def rim_rates(u):
    v, p, sound = primitives(u)
    total, along_y = None, None
    for d, (axis, step, size) in enumerate(((0, 2, 8), (1, 8, 384), (1, 1, 384))):
        flux, speed = directional(u, v, p, sound, d)

        def up(a):
            return pltpu.roll(a, size - step, axis)

        g = faces(u, [up(a) for a in u], flux, [up(a) for a in flux], speed, up(speed))
        div = [a - pltpu.roll(a, step, axis) for a in g]
        total = div if total is None else [a + b for a, b in zip(total, div)]
        along_y = g
    return total, along_y


def block_rates(src, edge, r0):
    lane = lax.broadcasted_iota(jnp.int32, (BLOCK, 8, 128), 2)
    odd = lax.broadcasted_iota(jnp.int32, (BLOCK, 8, 128), 1) % 2 == 1
    last = lane == 127
    base = pl.multiple_of(8 * (r0 - 1), 8)
    wide = [src[f, pl.ds(base, 8 * BLOCK + 16), :].reshape(BLOCK + 2, 8, 128) for f in range(5)]
    v, p, sound = primitives(wide)
    flux, speed = directional(wide, v, p, sound, 1)
    g = faces(
        [a[:-1] for a in wide], [a[1:] for a in wide], [a[:-1] for a in flux], [a[1:] for a in flux], speed[:-1], speed[1:]
    )
    total = [a[1:] - a[:-1] for a in g]
    u = [a[1:-1] for a in wide]
    v = [a[1:-1] for a in v]
    p, sound = p[1:-1], sound[1:-1]

    flux, speed = directional(u, v, p, sound, 0)

    def up_z(a):
        return pltpu.roll(a, 6, 1)

    g = faces(u, [up_z(a) for a in u], flux, [up_z(a) for a in flux], speed, up_z(speed))
    total = [t + (a - pltpu.roll(a, 2, 1)) for t, a in zip(total, g)]

    flux, speed = directional(u, v, p, sound, 2)

    def up_y(a):
        near = pltpu.roll(a, 127, 2)
        return jnp.where(last, pltpu.roll(near, 7, 1), near)

    g = faces(u, [up_y(a) for a in u], flux, [up_y(a) for a in flux], speed, up_y(speed))
    at = pl.multiple_of(8 * r0, 8)
    for f in range(5):
        outer = edge[f, pl.ds(at, 8 * BLOCK), :].reshape(BLOCK, 8, 128)
        upper = jnp.where(last & odd, outer, g[f])
        wrapped = jnp.where(odd, pltpu.roll(g[f], 1, 1), outer)
        lower = pltpu.roll(jnp.where(last, wrapped, g[f]), 1, 2)
        total[f] = total[f] + (upper - lower)
    return total


def kernel(
    density_h, velocity_h, pressure_h, lift_h, pointwise_h, project_h, spectral_h,
    fdj_h, fjd_h, inv_h, cx_h, cxt_h, pool_h,
    new_state_h, t_out,
    density, velocity, pressure, lift, pointwise, project, new_state, lift_wide,
    spectral, fdj, fjd, inv, cx, cxt, pool,
    u0, ua, ub, uc, acc, edge, rim, own_edge, side_edge, row_edge, corner_edge,
    pooled, snd_in, rcv_in, snd_tg, rcv_tg, snd_x, rcv_x, snd_b, rcv_b, snd_g, rcv_g,
    contracted, modes, grads, rt, slope, made, dp_hi, dp_lo, ft, lpx_ref, pxt_ref,
    load_sem, halo_send, halo_recv, in_send, in_recv, tg_send, tg_recv, x_send, x_recv, b_send, b_recv,
    g_send, g_recv, relay, xm_send, xm_recv, gm_send, gm_recv,
):
    ga = lax.axis_index("ga")
    dev = lax.axis_index("dev")
    east, west = lax.rem(ga + 1, GA), lax.rem(ga + GA - 1, GA)
    south, north = lax.rem(dev + 1, DEV), lax.rem(dev + DEV - 1, DEV)

    loads = [
        pltpu.make_async_copy(a, b, load_sem.at[n])
        for n, (a, b) in enumerate(
            (
                (pool_h, pool), (spectral_h, spectral), (fdj_h, fdj), (cx_h, cx), (cxt_h, cxt), (inv_h, inv), (fjd_h, fjd),
                (density_h, density), (velocity_h, velocity), (pressure_h, pressure),
                (lift_h, lift), (pointwise_h, pointwise), (project_h, project),
            )
        )
    ]
    for n in (7, 8, 9, 0, 10, 11, 12, 1, 2, 3, 4, 5, 6):
        loads[n].start()

    barrier = pltpu.get_barrier_semaphore()

    core, chip_x, chip_y = lax.rem(dev, 2), lax.rem(lax.div(dev, 2), 4), lax.div(dev, 8)

    def at(dy, dx, dc):
        return lax.rem(chip_y + dy, 4) * 8 + lax.rem(chip_x + dx, 4) * 2 + lax.rem(core + dc, 2)

    beside = jnp.where(core == 1, south, north)
    line_x = [(ga, at(0, k, 0)) for k in range(1, 4)]
    first = [(lax.rem(ga + k, GA), dev) for k in range(1, GA)]
    first += [(ga, at(a, 0, c)) for a in range(4) for c in range(2) if a + c] + line_x + [(ga, beside)]
    for who in first:
        pl.semaphore_signal(barrier, inc=1, device_id=who, device_id_type=MESH)

    def exchange_rows(snd, rcv, ssem, rsem, unit):
        for dy, dx, dc in OFFSETS:
            peer = at(dy, dx, dc)
            pltpu.make_async_remote_copy(
                src_ref=snd.at[pl.ds(pl.multiple_of(unit * peer, unit), unit)],
                dst_ref=rcv.at[pl.ds(pl.multiple_of(unit * dev, unit), unit)],
                send_sem=ssem.at[0], recv_sem=rsem.at[0],
                device_id=(ga, peer), device_id_type=MESH,
            ).start()
        mine = pl.ds(pl.multiple_of(unit * dev, unit), unit)
        rcv[mine, :] = snd[mine, :]

    def wait_rows(snd, rcv, ssem, rsem, unit):
        whole = pl.ds(0, unit * (DEV - 1))
        pltpu.make_async_remote_copy(
            src_ref=snd.at[whole], dst_ref=rcv.at[whole], send_sem=ssem.at[0], recv_sem=rsem.at[0],
            device_id=(ga, south), device_id_type=MESH,
        ).wait()

    def start_across(src, dst, ssem, rsem):
        for k in (2, 1, 3):
            peer = lax.rem(ga + k, GA)
            pltpu.make_async_remote_copy(
                src_ref=src(peer), dst_ref=dst.at[ga], send_sem=ssem.at[0], recv_sem=rsem.at[0],
                device_id=(peer, dev), device_id_type=MESH,
            ).start()

    def wait_across(src, dst, ssem, rsem):
        three = dst.at[pl.ds(0, GA - 1)]
        pltpu.make_async_remote_copy(
            src_ref=three, dst_ref=three, send_sem=ssem.at[0], recv_sem=rsem.at[0],
            device_id=(east, dev), device_id_type=MESH,
        ).wait()

    def coarsen(rows, snd):
        hi, lo = split2(rows)
        pooled[...] = nn(hi, pool[...]) + nn(lo, pool[...])
        both = pooled[pl.ds(0, 192, stride=2), :] + pooled[pl.ds(1, 192, stride=2), :]
        snd[...] = both.reshape(GA, 48, 128)

    for n in (7, 8, 9):
        loads[n].wait()
    for p in range(4):
        for h in range(2):
            cols = slice(128 * h, 128 * h + 128)
            rho = density[p, :, cols]
            v = [velocity[c, p, :, cols] for c in range(3)]
            where = pl.ds(32 + 2 * p + h, 32, stride=8)
            u0[0, where, :] = rho
            for c in range(3):
                u0[1 + c, where, :] = rho * v[c]
            u0[4, where, :] = pressure[p, :, cols] / 0.4 + 0.5 * rho * (v[0] * v[0] + v[1] * v[1] + v[2] * v[2])

    lane1 = lax.broadcasted_iota(jnp.int32, (8, 128), 1)
    for w in range(2):
        for f in range(5):
            packed = None
            for k in range(16):
                row = pltpu.roll(u0[f, pl.ds(8 * (16 * w + k + 4), 8), :], (4 + 8 * k) % 128, 1)
                packed = row if packed is None else jnp.where(lane1 >= 8 * k, row, packed)
            own_edge[w, f] = packed

    loads[0].wait()
    coarsen(jnp.concatenate([velocity[c, p] for p in range(4) for c in range(3)], axis=0), snd_in)

    pl.semaphore_wait(barrier, len(first))
    second = line_x + [(east, dev), (west, dev)]
    for who in second:
        pl.semaphore_signal(relay, inc=1, device_id=who, device_id_type=MESH)

    def halo(n, src, dst, target):
        return pltpu.make_async_remote_copy(
            src_ref=src, dst_ref=dst, send_sem=halo_send.at[n], recv_sem=halo_recv.at[n],
            device_id=target, device_id_type=MESH,
        )

    halos = [
        halo(0, u0.at[:, pl.ds(8 * 32, 32)], u0.at[:, pl.ds(0, 32)], (ga, south)),
        halo(0, u0.at[:, pl.ds(8 * 4, 32)], u0.at[:, pl.ds(8 * 36, 32)], (ga, north)),
        halo(2, own_edge, side_edge.at[0], (east, dev)),
        halo(2, own_edge, side_edge.at[1], (west, dev)),
        halo(1, own_edge.at[1], row_edge.at[0], (ga, south)),
        halo(1, own_edge.at[0], row_edge.at[1], (ga, north)),
    ]
    corners = [
        halo(3, own_edge.at[1], corner_edge.at[0], (east, south)),
        halo(3, own_edge.at[0], corner_edge.at[1], (east, north)),
        halo(3, own_edge.at[1], corner_edge.at[2], (west, south)),
        halo(3, own_edge.at[0], corner_edge.at[3], (west, north)),
    ]
    halo_waits = [
        halo(n, a, a, (ga, south)) for n, a in enumerate((u0.at[:, pl.ds(0, 64)], row_edge, side_edge, corner_edge))
    ]
    in_args = (lambda g: snd_in.at[g], rcv_in, in_send, in_recv)
    start_across(*in_args)
    for c in halos:
        c.start()
    rcv_in[ga] = snd_in[ga]

    for n in (10, 11, 12, 1):
        loads[n].wait()
    for c in range(3):
        lift_wide[c] = widened(lift[...], c)
    for ky in range(2):
        for part in range(2):

            def add(w8, total, ky=ky, part=part):
                total = list(total)
                for n in range(4):
                    w = 4 * w8 + n
                    s = spectral[ky, part, w].astype(F32)
                    for c in range(3):
                        total[c] = total[c] + jnp.broadcast_to(lift_wide[c, pl.ds(w, 1), :], (WIDTH, 128)) * s
                return tuple(total)

            zero = jnp.zeros((WIDTH, 128), F32)
            done = lax.fori_loop(0, WIDTH // 4, add, (zero, zero, zero))
            for c in range(3):
                contracted[ky, part, c] = done[c]

    tile_o = (
        lax.broadcasted_iota(jnp.int32, (WIDTH, 512), 1) % WIDTH == lax.broadcasted_iota(jnp.int32, (WIDTH, 512), 0)
    ).astype(F32).astype(BF16)
    same_row = (
        lax.broadcasted_iota(jnp.int32, (48, 512), 1) // WIDTH == lax.broadcasted_iota(jnp.int32, (48, 512), 0) % 16
    )

    def spread(a):
        return jnp.where(
            same_row, jnp.concatenate([jnp.broadcast_to(a[c : c + 1], (16, 512)) for c in range(3)], axis=0), 0.0
        )

    lp_hi, lp_lo = split2(nn(lift[...], pointwise[...]))
    lpx_ref[...] = spread(nn(lp_hi, tile_o) + nn(lp_lo, tile_o))
    spread_out = jnp.concatenate([spread(nn(project[...], tile_o)), jnp.zeros((80, 512), F32)], axis=0)
    pxt_ref[...] = jnp.concatenate([spread_out, spread_out], axis=0).astype(BF16)

    pl.semaphore_wait(relay, len(second))
    for c in corners:
        c.start()

    wait_across(*in_args)
    loads[2].wait()
    hi, lo = split2(jnp.concatenate([rcv_in[g] for g in range(GA)], axis=1))
    freq = nt(hi, fdj[0]) + nt(hi, fdj[1]) + nt(lo, fdj[0])
    for d in range(DEV):
        packed = None
        for n in range(6):
            h, c = n // 3, n % 3
            piece = pltpu.roll(freq[16 * c + 8 * h : 16 * c + 8 * h + 8], (16 * h + 4 * c - 4 * d) % 128, 1)
            packed = piece if packed is None else jnp.where(lane1 >= 16 * h + 4 * c, piece, packed)
        snd_x[pl.ds(8 * d, 8), :] = packed
    x_args = (snd_x, rcv_x, x_send, x_recv, 8)
    exchange_rows(*x_args)

    sub1 = lax.broadcasted_iota(jnp.int32, (8, 128), 0)
    even, outside = sub1 % 2 == 0, lane1 % 8 < 4
    low = lane1 < 64

    def fill_rim(n, f, own, left, right):
        rim[0, f, :, 128 * n : 128 * n + 128] = jnp.where(
            even, jnp.where(outside, pltpu.roll(left, 7, 0), own), jnp.where(outside, own, pltpu.roll(right, 1, 0))
        )

    def stage(src, dst, ahead, first_row, last_row, rim_src, rim_dst, stride=BLOCK):
        total, along_y = rim_rates([rim[rim_src, f] for f in range(5)])
        for f in range(5):
            if rim_dst is not None:
                rim[rim_dst, f] = rim[0, f] - (0.5 * ahead) * total[f]
            for n in range(3):
                for k in range(16):
                    edge[f, pl.ds(8 * ((16 * n + k + 4) % 48), 8), :] = pltpu.roll(
                        along_y[f][:, 128 * n : 128 * n + 128], 124 - 8 * k, 1
                    )

        def block(n, carry):
            r0 = jnp.minimum(first_row + stride * n, last_row + 1 - BLOCK)
            total = block_rates(src, edge, r0)
            at = pl.ds(pl.multiple_of(8 * r0, 8), 8 * BLOCK)
            for f in range(5):
                t = total[f].reshape(8 * BLOCK, 128)
                if dst is not None:
                    dst[f, at, :] = u0[f, at, :] - (0.5 * ahead) * t
                else:
                    mean = (ua[f, at, :] + 2.0 * ub[f, at, :] + uc[f, at, :] - u0[f, at, :]) * (1.0 / 3.0)
                    acc[f, at, :] = mean - (DT / 12.0) * t
            return carry

        lax.fori_loop(0, -(-(last_row + 1 - first_row) // stride), block, 0)

    halo_waits[2].wait()
    for f in range(5):
        for n in range(2):
            fill_rim(n, f, own_edge[n, f], side_edge[0, n, f], side_edge[1, n, f])
        fill_rim(2, f, own_edge[0, f], side_edge[0, 0, f], side_edge[1, 0, f])
    stage(u0, ua, 0.5 * DT, 5, 34, 0, None)
    for n in (0, 1, 3):
        halo_waits[n].wait()
    for f in range(5):
        fill_rim(
            2, f, jnp.where(low, row_edge[1, f], row_edge[0, f]),
            jnp.where(low, corner_edge[1, f], corner_edge[0, f]), jnp.where(low, corner_edge[3, f], corner_edge[2, f]),
        )
    stage(u0, ua, 0.5 * DT, 1, 38, 0, 1, 30)
    stage(ua, ub, 0.5 * DT, 2, 37, 1, 2)

    wait_rows(*x_args)
    loads[3].wait()
    hi, lo = split2(rcv_x[...])
    turned = 0.0
    for h in range(2):
        cols = slice(256 * h, 256 * h + 256)
        half = nn(cx[0, :, cols], hi) + nn(cx[1, :, cols], hi) + nn(cx[0, :, cols], lo)
        turned = turned + (pltpu.roll(half, 112, 1) if h else half)
    cosine, sine = turned[:128].T, turned[128:].T
    for ky in range(2):
        for c in range(3):
            r = 4 * c + 2 * ky
            modes[ga, 8 * ky + 2 * c : 8 * ky + 2 * c + 1, :] = cosine[r : r + 1] + sine[r + 1 : r + 2]
            modes[ga, 8 * ky + 2 * c + 1 : 8 * ky + 2 * c + 2, :] = cosine[r + 1 : r + 2] - sine[r : r + 1]
        modes[ga, 8 * ky + 6 : 8 * ky + 8, :] = jnp.zeros((2, 128), F32)
    modes_args = (lambda g: modes.at[ga], modes, xm_send, xm_recv)
    start_across(*modes_args)
    mine = modes[ga]
    rows = []
    for ky in range(2):
        out_re, out_im = 0.0, 0.0
        for c in range(3):
            a = mine[8 * ky + 2 * c : 8 * ky + 2 * c + 1]
            b = mine[8 * ky + 2 * c + 1 : 8 * ky + 2 * c + 2]
            re, im = contracted[ky, 0, c], contracted[ky, 1, c]
            out_re = out_re + (a * re - b * im)
            out_im = out_im + (a * im + b * re)
        rows.append(jnp.concatenate([out_re, -out_im], axis=1))
        rows.append(jnp.concatenate([out_im, out_re], axis=1))
    hi, lo = split2(jnp.concatenate(rows, axis=0))
    loads[4].wait()
    snd_b[...] = nt(cxt[0], hi) + nt(cxt[1], hi) + nt(cxt[0], lo)
    b_args = (snd_b, rcv_b, b_send, b_recv, 16)
    exchange_rows(*b_args)

    stage(ub, uc, DT, 3, 36, 2, 1)
    stage(uc, None, DT, 4, 35, 1, None)

    after = []
    for p in range(4):
        parts = []
        for h in range(2):
            where = pl.ds(32 + 2 * p + h, 32, stride=8)
            u = [acc[f, where, :] for f in range(5)]
            inv_rho = 1.0 / u[0]
            parts.append([u[1 + c] * inv_rho for c in range(3)])
        for c in range(3):
            after.append(jnp.concatenate([parts[0][c], parts[1][c]], axis=1))
    coarsen(jnp.concatenate(after, axis=0), snd_tg)
    tg_args = (lambda g: snd_tg.at[g], rcv_tg, tg_send, tg_recv)
    start_across(*tg_args)
    rcv_tg[ga] = snd_tg[ga]
    for p in range(4):
        for h in range(2):
            for f in range(5):
                new_state[f, p, :, 128 * h : 128 * h + 128] = acc[f, pl.ds(32 + 2 * p + h, 32, stride=8), :]
    state_copy = pltpu.make_async_copy(new_state, new_state_h, load_sem.at[13])
    state_copy.start()

    lpx_hi, lpx_lo = split2(lpx_ref[...])

    def transposed(a):
        return jnp.concatenate([a, jnp.zeros((80, 128), F32)], axis=0).T

    for g in range(GA):
        ins_hi, ins_lo = split2(transposed(rcv_in[g])[:, :48])
        slope[pl.ds(128 * g, 128), :] = nn(ins_hi, lpx_hi) + nn(ins_hi, lpx_lo) + nn(ins_lo, lpx_hi)

    wait_rows(*b_args)
    loads[5].wait()
    group = lax.broadcasted_iota(jnp.int32, (32, 128), 1) // 32
    for t in range(4):
        src = [rcv_b[pl.ds(4 * t + m, 32, stride=16), :] for m in range(4)]
        for j in range(4):
            made_of = None
            for m in range(4):
                turn = (32 * (m - j)) % 128
                piece = pltpu.roll(src[m], turn, 1) if turn else src[m]
                made_of = piece if made_of is None else jnp.where(group == m, piece, made_of)
            hi, lo = split2(made_of)
            for n, piece in enumerate((hi, lo, hi)):
                rt[pl.ds(128 * n + 32 * j, 32), 128 * t : 128 * t + 128] = piece

    k0, k1 = math.sqrt(2.0 / math.pi), 0.044715

    def forward(g, carry):
        at = pl.ds(pl.multiple_of(128 * g, 128), 128)
        pre = slope[at, :] + nn(inv[at, :], rt[...])
        square = pre * pre
        t = jnp.tanh(k0 * pre * (1.0 + k1 * square))
        half = 0.5 * (1.0 + t)
        slope[at, :] = half + (0.5 * k0) * pre * (1.0 - t * t) * (1.0 + (3.0 * k1) * square)
        hi, lo = split2(pre * half)
        made[at, :] = nt(hi, pxt_ref[:128]) + nt(lo, pxt_ref[:128])
        return carry

    lax.fori_loop(0, GA, forward, 0, unroll=True)

    wait_across(*tg_args)

    def backward(g, carry):
        at = pl.ds(pl.multiple_of(128 * g, 128), 128)
        hi, lo = split2(made[at, :] - transposed(rcv_tg[g]))
        d_pre = nn(jnp.concatenate([hi, lo], axis=1), pxt_ref[...]) * slope[at, :]
        hi, lo = split2(d_pre)
        dp_hi[at, :] = hi
        dp_lo[at, :] = lo
        return carry

    lax.fori_loop(0, GA, backward, 0, unroll=True)
    loads[6].wait()
    for t in range(2):
        cols = slice(256 * t, 256 * t + 256)
        both = nn(fjd[0], dp_hi[:, cols]) + nn(fjd[1], dp_hi[:, cols]) + nn(fjd[0], dp_lo[:, cols])
        ft[2 * t], ft[2 * t + 1] = both[:, :128], both[:, 128:]
    for t in range(4):
        src = [ft[t, pl.ds(32 * j, 32), :] for j in range(4)]
        for m in range(4):
            made_of = None
            for j in range(4):
                turn = (32 * (j - m)) % 128
                piece = pltpu.roll(src[j], turn, 1) if turn else src[j]
                made_of = piece if made_of is None else jnp.where(group == j, piece, made_of)
            snd_g[pl.ds(4 * t + m, 32, stride=16), :] = made_of
    g_args = (snd_g, rcv_g, g_send, g_recv, 16)
    exchange_rows(*g_args)
    wait_rows(*g_args)

    arrived = rcv_g[...].reshape(DEV, 2, 8, 128)
    hi, lo = split2(jnp.concatenate([arrived[:, h].reshape(256, 128) for h in range(2)], axis=0))
    turned = nn(cx[0], hi) + nn(cx[1], hi) + nn(cx[0], lo)
    cosine, sine = turned[:128].T, turned[128:].T
    for ky in range(2):
        re, im = slice(64 * ky, 64 * ky + 32), slice(64 * ky + 32, 64 * ky + 64)
        grads[ga, ky, 0] = cosine[re] + sine[im]
        grads[ga, ky, 1] = cosine[im] - sine[re]
    grads_args = (lambda g: grads.at[ga], grads, gm_send, gm_recv)
    start_across(*grads_args)
    wait_across(*modes_args)
    wait_across(*grads_args)
    for ky in range(2):
        factor = jnp.where(2 * dev + ky == 0, 1.0, 2.0).astype(F32) / (XC * YC)
        for c in range(3):
            out_re, out_im = 0.0, 0.0
            for b in range(GA):
                x_re = modes[b, 8 * ky + 2 * c : 8 * ky + 2 * c + 1, :]
                x_im = modes[b, 8 * ky + 2 * c + 1 : 8 * ky + 2 * c + 2, :]
                g_re, g_im = grads[b, ky, 0], grads[b, ky, 1]
                out_re = out_re + (x_re * g_re + x_im * g_im)
                out_im = out_im + (x_re * g_im - x_im * g_re)
            t_out[ky, 0, c] = out_re * factor
            t_out[ky, 1, c] = out_im * factor
    state_copy.wait()


def expand_kernel(lift_h, t_h, state_h, out_h, new_state_h, lift, t, state, lift_wide, out, sem):
    loads = [
        pltpu.make_async_copy(a, b, sem.at[n]) for n, (a, b) in enumerate(((lift_h, lift), (t_h, t), (state_h, state)))
    ]
    for c in loads:
        c.start()
    forward = pltpu.make_async_copy(state, new_state_h, sem.at[4])
    loads[0].wait()
    for c in range(3):
        lift_wide[c] = widened(lift[...], c)
    loads[1].wait()

    def stretch(n):
        ky, rest = n // 8, n % 8
        part, rows = rest // 4, pl.ds(8 * (rest % 4), 8)
        return pltpu.make_async_copy(out.at[ky, part, rows], out_h.at[ky, part, rows], sem.at[3])

    def body(n, carry):
        ky, rest = n // 8, n % 8
        part, first = rest // 4, 8 * (rest % 4)
        terms = [t[ky, part, c] for c in range(3)]
        for i in range(8):
            total = 0.0
            for c in range(3):
                total = total + jnp.broadcast_to(lift_wide[c, pl.ds(first + i, 1), :], (WIDTH, 128)) * terms[c]
            out[ky, part, first + i] = total
        stretch(n).start()
        return carry

    lax.fori_loop(0, 4, body, 0)
    loads[2].wait()
    forward.start()
    lax.fori_loop(4, 16, body, 0)

    pltpu.make_async_copy(out, out_h, sem.at[3]).wait()
    forward.wait()


def per_device(consts, density, velocity, pressure, lift, spectral, pointwise, project):
    hbm = pl.BlockSpec(memory_space=pl.ANY)
    V = pltpu.VMEM
    dma = pltpu.SemaphoreType.DMA
    field = V((5, 384, 128), F32)
    rows = V((512, 128), F32)
    coarse = V((GA, 48, 128), F32)
    scratch = [
        V((4, 32, 256), F32), V((3, 4, 32, 256), F32), V((4, 32, 256), F32), V((3, WIDTH), BF16), V((WIDTH, WIDTH), BF16),
        V((3, WIDTH), BF16), V((5, 4, 32, 256), F32), V((3, WIDTH, 128), F32),
        V((2, 2, WIDTH, WIDTH, 128), BF16), V((2, 128, 512), BF16), V((2, 128, 512), BF16), V((512, 384), BF16),
        V((2, 256, 512), BF16), V((2, 512, 256), BF16), V((256, 128), BF16),
        field, field, field, field, field, field, V((3, 5, 8, 384), F32),
        V((2, 5, 8, 128), F32), V((2, 2, 5, 8, 128), F32), V((2, 5, 8, 128), F32), V((4, 5, 8, 128), F32),
        V((384, 128), F32), coarse, coarse, coarse, coarse, V((256, 128), F32), V((256, 128), F32), rows, rows, rows, rows,
        V((2, 2, 3, WIDTH, 128), F32), V((GA, 16, 128), F32), V((GA, 2, 2, WIDTH, 128), F32),
        V((384, 512), BF16), V((512, 512), F32), V((512, 128), F32),
        V((512, 512), BF16), V((512, 512), BF16), V((4, 128, 128), F32), V((48, 512), F32), V((256, 512), BF16),
        dma((14,)), dma((4,)), dma((4,)), dma((1,)), dma((1,)), dma((1,)), dma((1,)),
        dma((1,)), dma((1,)), dma((1,)), dma((1,)), dma((1,)), dma((1,)),
        pltpu.SemaphoreType.REGULAR, dma((1,)), dma((1,)), dma((1,)), dma((1,)),
    ]
    new_state, t = pl.pallas_call(
        kernel,
        out_shape=(
            jax.ShapeDtypeStruct((5, 4, 32, 256), F32),
            jax.ShapeDtypeStruct((2, 2, 3, WIDTH, 128), F32),
        ),
        in_specs=[hbm] * 13,
        out_specs=(hbm, pl.BlockSpec(memory_space=pltpu.VMEM)),
        scratch_shapes=scratch,
        compiler_params=pltpu.CompilerParams(
            collective_id=0, has_side_effects=True, vmem_limit_bytes=VMEM_BYTES
        ),
    )(density, velocity, pressure, lift, pointwise, project.T, spectral, *consts)
    grad, new_state = pl.pallas_call(
        expand_kernel,
        out_shape=(
            jax.ShapeDtypeStruct((2, 2, WIDTH, WIDTH, 128), F32),
            jax.ShapeDtypeStruct((5, 4, 32, 256), F32),
        ),
        in_specs=[hbm] * 3,
        out_specs=(hbm, hbm),
        scratch_shapes=[
            V((3, WIDTH), BF16), V((2, 2, 3, WIDTH, 128), F32), V((5, 4, 32, 256), F32), V((3, WIDTH, 128), F32),
            V((2, 2, WIDTH, WIDTH, 128), F32), dma((5,)),
        ],
        compiler_params=pltpu.CompilerParams(vmem_limit_bytes=VMEM_BYTES),
    )(lift, t, new_state)
    return new_state, grad


def solution(mesh):
    in_specs = (
        P(None, "dev", "ga"),
        P(None, None, "dev", "ga"),
        P(None, "dev", "ga"),
        P(),
        P("dev", None, None, None, None),
        P(),
        P(),
    )
    out_specs = (P(None, None, "dev", "ga"), P("dev", None, None, None, None))

    def whole(*args):
        consts = tables()
        return jax.shard_map(
            lambda *a: per_device(a[:6], *a[6:]),
            mesh=mesh, in_specs=(P(),) * 6 + in_specs, out_specs=out_specs, check_vma=False,
        )(*[jnp.asarray(c) for c in consts], *args)

    return whole
```
